512 devices in a mesh: dp: 16 (over z, core), cell: 32 (over x, y).
Axes of the slice: x: 4, y: 8, z: 8, core: 2. Of those that a mesh axis runs over, the one named last changes fastest.
Arguments:
- configs: int32 [2048, 4], P('dp'), may hold values from 0 to 2047, all different within a row
- pole_fields: bfloat16 [3, 2048, 32768], P(None, 'dp', 'cell'), may hold values from -3 to 3
- misfit: float32 [2048], P('dp'), may hold values from -6 to 6
- data_weight: float32 [2048], P('dp'), may hold values from 0.3 to 3
- conductivity: float32 [32768], P('cell'), may hold values from -6 to 6
- face_weights: float32 [3, 32768], P(None, 'cell'), may hold values from 0.05 to 0.5
Outputs:
- update: float32 [32768], P('cell')
- data_change: float32 [2048], P('dp')
The draws below stay inside these ranges and needn't reach their ends.
Inputs may be any that keep to these rules, and one draw needn't show every extreme that they name: `configs`: each row names four different poles.
All inputs are finite; a program needn't handle non-finite values.
Results may differ from the reference program's by a relative error of at most 0.0003.
Values may be sent and summed in bfloat16 or wider, within the bound.
A program may use at most 64 MiB of HBM per device.

```python
import math
import jax
import jax.numpy as jnp
from jax import lax

POLES = 2048
GY = 32
GZ = 32
ITERS = 3
DATA = 2048
NX = 32
CELLS = 32768


def block_levels(rng, extent, shards, smallest, top_value):
    def one(axis_at, shards_of):
        draws = jax.random.uniform(jax.random.fold_in(jax.random.fold_in(rng, 6), axis_at), (shards_of,), jnp.float32, smallest / len(shards), top_value / len(shards))
        return jnp.repeat(jnp.exp(draws), extent[axis_at] // shards_of).reshape((-1,) + (1,) * (len(extent) - axis_at - 1))

    gain = one(*shards[0])
    for cut in shards[1:]:
        gain = gain * one(*cut)
    return gain


def choose_distinct(stream_key, rows, number_of, top, lift):
    sequence = jax.random.permutation(jax.random.fold_in(stream_key, 1), number_of)
    pull = sequence
    for power in range(3):
        pull = pull * pull // number_of
    pull = pull * lift // number_of
    chance = jax.random.randint(jax.random.fold_in(stream_key, 2), (rows, number_of), 0, 4096) + pull
    holders = jax.random.permutation(jax.random.fold_in(stream_key, 3), rows)[jnp.arange(number_of) % rows]
    chance = jnp.where(jnp.arange(rows)[:, None] == holders[None, :], 1 << 14, chance)
    merit = chance * number_of + jnp.arange(number_of)
    return lax.top_k(merit.astype(jnp.int32), top)[1].astype(jnp.int32)


def bell_draw(stream_key, shape, spread, limit, split=(), dtype=jnp.bfloat16):
    entries = spread * jax.random.normal(stream_key, shape, jnp.float32)
    if split:
        entries = entries * block_levels(stream_key, shape, split, -0.22, 0.18)
    return jnp.clip(entries, -limit, limit).astype(dtype)


def setup_inputs(seed: int = 0) -> dict:
    streams_of = jax.random.split(jax.random.key(seed), 7)
    return {
        "configs": choose_distinct(streams_of[0], DATA, POLES, 4, 0),
        "pole_fields": bell_draw(streams_of[1], (3, POLES, CELLS), 0.5, 3.0, ((1, 16), (2, 32))),
        "misfit": bell_draw(streams_of[2], (DATA,), 1.0, 6.0, ((0, 16),), jnp.float32),
        "data_weight": jnp.clip(jnp.exp(math.log(3.0) - 2.3025851 * jax.random.uniform(streams_of[3], (DATA,), jnp.float32) ** block_levels(streams_of[3], (DATA,), ((0, 16),), -0.2, 0.2)), 0.3, 3.0),
        "conductivity": bell_draw(streams_of[4], (CELLS,), 1.0, 6.0, ((0, 32),), jnp.float32),
        "face_weights": jnp.clip(jnp.exp(math.log(0.5) - 2.3025851 * jax.random.uniform(streams_of[5], (3, CELLS), jnp.float32) ** block_levels(streams_of[5], (3, CELLS), ((1, 32),), -0.2, 0.2)), 0.05, 0.5),
    }


DAMPING = 0.2

def roughness(vector, face_weights):
    grid = vector.reshape(NX, GY, GZ)
    weights = face_weights.reshape(3, NX, GY, GZ)
    result = jnp.zeros((NX, GY, GZ), jnp.float32)
    flux = weights[0, :-1] * (grid[1:] - grid[:-1])
    result = result.at[:-1].add(-flux).at[1:].add(flux)
    flux = weights[1][:, :-1] * (grid[:, 1:] - grid[:, :-1])
    result = result.at[:, :-1].add(-flux).at[:, 1:].add(flux)
    flux = weights[2][:, :, :-1] * (grid[:, :, 1:] - grid[:, :, :-1])
    result = result.at[:, :, :-1].add(-flux).at[:, :, 1:].add(flux)
    return result.reshape(-1)

def sensitivity_matrix(configs, pole_fields):
    totals = jnp.zeros((DATA, CELLS), jnp.float32)
    for component in range(3):
        fields = pole_fields[component].astype(jnp.float32)
        source = fields[configs[:, 0]] - fields[configs[:, 1]]
        receiver = fields[configs[:, 2]] - fields[configs[:, 3]]
        totals = totals + source * receiver
    return -totals / math.sqrt(DATA)

def reference(configs, pole_fields, misfit, data_weight, conductivity, face_weights):
    high = lax.Precision.HIGHEST
    sensitivity = sensitivity_matrix(configs, pole_fields)

    def apply_hessian(vector):
        predicted = jnp.dot(sensitivity, vector, precision=high)
        return jnp.dot(data_weight * predicted, sensitivity, precision=high) + roughness(vector, face_weights) + DAMPING * vector
    gradient = jnp.dot(data_weight * misfit, sensitivity, precision=high) - roughness(conductivity, face_weights)
    update = jnp.zeros_like(gradient)
    residual = gradient
    direction = gradient
    norm_now = jnp.sum(residual * residual)
    for iteration in range(ITERS):
        image = apply_hessian(direction)
        step_length = norm_now / jnp.sum(direction * image)
        update = update + step_length * direction
        residual = residual - step_length * image
        norm_next = jnp.sum(residual * residual)
        direction = residual + norm_next / norm_now * direction
        norm_now = norm_next
    data_change = jnp.dot(sensitivity, update, precision=high)
    return (update, data_change)
```

```python
import functools
import math

import jax
import jax.numpy as jnp
from jax import lax
from jax.experimental import pallas as pl
from jax.experimental.pallas import tpu as pltpu
from jax.sharding import PartitionSpec as P

GY = 32
GZ = 32
ITERS = 3
DAMPING = 0.2

DP = 16
CELL = 32
OWN = 64
POLE_ROWS = 128
CHUNK = 256
DATA = 2048
LANES = 128
F32 = jnp.float32
BF16 = jnp.bfloat16
MESH = pl.DeviceIdType.MESH


def lane_sum(row):
    return jnp.sum(row, axis=1, keepdims=True)


def kernel(
    fields,
    configs_t,
    misfit,
    weight,
    conductivity,
    faces,
    update_out,
    change_out,
    field_out,
    field_in,
    signs,
    totals,
    sens,
    setup_out,
    setup_in,
    static_out,
    static_in,
    first_out,
    first_in,
    plane_out,
    plane_in,
    second_out,
    second_in,
    third_in,
    field_send,
    field_recv,
    send_sems,
    recv_sems,
):
    dp = lax.axis_index("dp")
    cell = lax.axis_index("cell")
    chip = dp // 2
    core = dp % 2
    above = (cell + 1) % CELL
    below = (cell + CELL - 1) % CELL

    barrier = pltpu.get_barrier_semaphore()
    for step in range(1, DP):
        pl.semaphore_signal(
            barrier, inc=1, device_id={"dp": (dp + step) % DP, "cell": cell}, device_id_type=MESH
        )
    for step in range(1, CELL):
        pl.semaphore_signal(
            barrier, inc=1, device_id={"dp": dp, "cell": (cell + step) % CELL}, device_id_type=MESH
        )

    lane = lax.broadcasted_iota(jnp.int32, (1, LANES), 1)
    own = (lane >= 32) & (lane < 96)

    for target in range(8):
        for part in range(3):
            turned = fields[part, :, target * LANES : (target + 1) * LANES].T
            field_out[2 * target, part * OWN : (part + 1) * OWN, :] = turned[:OWN]
            field_out[2 * target + 1, part * OWN : (part + 1) * OWN, :] = turned[OWN:]
    field_in[dp] = field_out[dp]

    setup_out[0:4, :] = configs_t[...].astype(F32)
    setup_out[4:5, :] = weight[...]
    setup_out[5:6, :] = misfit[...]
    setup_out[6:8, :] = jnp.zeros((2, LANES), F32)
    setup_in[dp] = setup_out[...]

    even = dp % 2 == 0
    tile_a = jnp.maximum((dp + 1) // 2 - 1, 0)
    tile_b = jnp.minimum((dp + 1) // 2, 7)

    def widened(first, second):
        if_even = jnp.where(lane < 32, pltpu.roll(first, 32, 1), pltpu.roll(second, 32, 1))
        if_odd = jnp.where(lane < 96, pltpu.roll(first, 96, 1), pltpu.roll(second, 96, 1))
        return jnp.where(jnp.broadcast_to(even, (1, LANES)), if_even, if_odd)

    def face_row(axis):
        return widened(
            faces[axis : axis + 1, pl.ds(pl.multiple_of(tile_a * LANES, LANES), LANES)],
            faces[axis : axis + 1, pl.ds(pl.multiple_of(tile_b * LANES, LANES), LANES)],
        )

    cond_row = widened(conductivity[pl.ds(tile_a, 1), :], conductivity[pl.ds(tile_b, 1), :])
    face_x, face_y, face_z = face_row(0), face_row(1), face_row(2)
    static_out[0:1, :] = cond_row
    static_out[1:2, :] = face_x

    totals[...] = jnp.zeros(totals.shape, F32)

    pl.semaphore_wait(barrier, DP - 1 + CELL - 1)

    def push(source, target, send, recv, to_dp, to_cell):
        pltpu.make_async_remote_copy(
            src_ref=source,
            dst_ref=target,
            send_sem=send,
            recv_sem=recv,
            device_id={"dp": to_dp, "cell": to_cell},
            device_id_type=MESH,
        ).start()

    def await_bytes(ref, sem):
        pltpu.make_async_copy(ref, ref, sem).wait()

    for step in range(1, DP):
        push(setup_out, setup_in.at[dp], send_sems.at[0], recv_sems.at[0], (dp + step) % DP, cell)
    push(static_out, static_in.at[0], send_sems.at[1], recv_sems.at[1], dp, above)
    push(static_out, static_in.at[1], send_sems.at[1], recv_sems.at[1], dp, below)
    for far in (4, 3, 5, 2, 6, 1, 7, 0):
        for other in (0, 1):
            if (far, other) == (0, 0):
                continue
            to = (chip + far) % 8 * 2 + (core + other) % 2
            push(field_out.at[to], field_in.at[dp], field_send, field_recv.at[dp], to, cell)

    await_bytes(setup_in.at[pl.ds(0, DP - 1)], recv_sems.at[0])

    def one_chunk(step, carry):
        half = (step + 1) // 2
        chunk = (chip + (8 - half) % 8 + (step % 2) * (2 * half - 8)) % 8
        ids = (lax.broadcasted_iota(jnp.int32, (CHUNK, 1), 0) + chunk * CHUNK).astype(F32)

        def signs_of(block, inner):
            rows = setup_in[block]
            at = pl.multiple_of(block * LANES, LANES)
            for pair in range(2):
                plus, minus = rows[2 * pair : 2 * pair + 1], rows[2 * pair + 1 : 2 * pair + 2]
                value = jnp.where(ids == plus, 1.0, jnp.where(ids == minus, -1.0, 0.0))
                signs[:, pl.ds(pl.multiple_of(pair * DATA + at, LANES), LANES)] = value.astype(BF16)
            return inner

        lax.fori_loop(0, DP, signs_of, 0)

        def wait_field(source):
            @pl.when(source != dp)
            def _():
                await_bytes(field_in.at[source], field_recv.at[source])

        wait_field(2 * chunk)
        wait_field(2 * chunk + 1)
        left = jnp.concatenate([field_in[2 * chunk], field_in[2 * chunk + 1]], axis=1)

        def product(tile, inner):
            at = pl.ds(pl.multiple_of(tile * 512, 512), 512)
            totals[:, at] += jnp.dot(left, signs[:, at], preferred_element_type=F32)
            return inner

        lax.fori_loop(0, 8, product, 0)
        return carry

    lax.fori_loop(0, 8, one_chunk, 0)

    scale = -1.0 / math.sqrt(DATA)
    gradient_sum = jnp.zeros((OWN, LANES), F32)
    for block in range(DP):
        at, bt = block * LANES, DATA + block * LANES
        value = totals[0:OWN, at : at + LANES] * totals[0:OWN, bt : bt + LANES]
        for part in (1, 2):
            rows = slice(part * OWN, (part + 1) * OWN)
            value += totals[rows, at : at + LANES] * totals[rows, bt : bt + LANES]
        value = value * scale
        sens[block] = value
        gradient_sum += value * (setup_in[block, 4:5, :] * setup_in[block, 5:6, :])

    spot = lax.broadcasted_iota(jnp.int32, (OWN, LANES), 0) + 32 == lax.broadcasted_iota(
        jnp.int32, (OWN, LANES), 1
    )

    def to_row(spread):
        column = jnp.sum(spread, axis=1, keepdims=True)
        return jnp.sum(jnp.where(spot, column, 0.0), axis=0, keepdims=True)

    def to_column(row):
        return jnp.sum(jnp.where(spot, row, 0.0), axis=1, keepdims=True)

    await_bytes(static_in, recv_sems.at[1])

    def masked(row, keep):
        return jnp.where(own & keep, row, 0.0)

    grid_y = 2 * dp + (lane - 32) // 32
    grid_z = lane % 32
    up_x = masked(face_x, jnp.broadcast_to(cell < CELL - 1, (1, LANES)))
    low_x = masked(static_in[0, 1:2, :], jnp.broadcast_to(cell > 0, (1, LANES)))
    up_y = masked(face_y, grid_y < GY - 1)
    low_y = masked(pltpu.roll(face_y, 32, 1), grid_y > 0)
    up_z = masked(face_z, grid_z < GZ - 1)
    low_z = masked(pltpu.roll(face_z, 1, 1), grid_z > 0)

    def roughness(row, lower, upper):
        return (
            up_x * (row - upper)
            + low_x * (row - lower)
            + up_y * (row - pltpu.roll(row, 96, 1))
            + low_y * (row - pltpu.roll(row, 32, 1))
            + up_z * (row - pltpu.roll(row, 127, 1))
            + low_z * (row - pltpu.roll(row, 1, 1))
        )

    residual = to_row(gradient_sum) - roughness(cond_row, static_in[0, 0:1, :], static_in[1, 0:1, :])
    residual = jnp.where(own, residual, 0.0)

    for it in range(ITERS):
        sem = 2 + 4 * it
        column = jnp.broadcast_to(to_column(residual), (OWN, LANES))
        plane_out[it] = residual
        push(plane_out.at[it], plane_in.at[it, 0], send_sems.at[sem], recv_sems.at[sem], dp, above)
        push(plane_out.at[it], plane_in.at[it, 1], send_sems.at[sem], recv_sems.at[sem], dp, below)
        for block in range(DP):
            image_row = jnp.sum(sens[block] * column, axis=0, keepdims=True)
            first_out[it, block] = jnp.concatenate([image_row, residual], axis=0)
        for step in (8, 7, 9, 6, 10, 5, 11, 4, 12, 3, 13, 2, 14, 1, 15):
            to = (dp + step) % DP
            push(
                first_out.at[it, to],
                first_in.at[it, dp],
                send_sems.at[sem + 1],
                recv_sems.at[sem + 1],
                to,
                cell,
            )
        first_in[it, dp] = first_out[it, dp]
        await_bytes(plane_in.at[it], recv_sems.at[sem])
        await_bytes(first_in.at[it, pl.ds(0, DP - 1)], recv_sems.at[sem + 1])
        gathered = first_in[it]
        partial = jnp.sum(gathered[:, 0:1, :], axis=0)
        before = first_in[it, (dp + DP - 1) % DP][1:2, :]
        after = first_in[it, (dp + 1) % DP][1:2, :]
        wide = jnp.where(
            own, residual, pltpu.roll(jnp.where(lane >= 64, before, after), 64, 1)
        )
        rough = roughness(wide, plane_in[it, 0], plane_in[it, 1]) + DAMPING * residual
        scalars = jnp.where(lane == 0, lane_sum(residual * residual), 0.0)
        scalars = jnp.where(lane == 1, lane_sum(residual * rough), scalars)
        if it > 0:
            scalars = jnp.where(lane == 2, lane_sum(residual * direction_rough), scalars)
        message = jnp.concatenate([partial, scalars], axis=0)
        second_out[it] = message
        for step in range(1, CELL):
            push(
                second_out.at[it],
                second_in.at[it, step - 1],
                send_sems.at[sem + 2],
                recv_sems.at[sem + 2],
                dp,
                (cell + step) % CELL,
            )
        await_bytes(second_in.at[it], recv_sems.at[sem + 2])
        message = message + jnp.sum(second_in[it], axis=0)
        third_in[it, dp] = message
        for step in (8, 7, 9, 6, 10, 5, 11, 4, 12, 3, 13, 2, 14, 1, 15):
            push(
                third_in.at[it, dp],
                third_in.at[it, dp],
                send_sems.at[sem + 3],
                recv_sems.at[sem + 3],
                (dp + step) % DP,
                cell,
            )
        await_bytes(third_in.at[it, pl.ds(0, DP - 1)], recv_sems.at[sem + 3])
        sums = jnp.sum(third_in[it][:, 1:2, :], axis=0)
        norm_next = sums[:, 0:1]
        energy = sums[:, 1:2]
        plane_rows = gathered[:, 1, :]
        if it == 0:
            predicted = [third_in[it, block][0:1, :] for block in range(DP)]
            direction_rough = rough
            predicted_own = message[0:1, :]
            whole = plane_rows
        else:
            ratio = norm_next / norm_now
            energy = energy + ratio * (2.0 * sums[:, 2:3] + ratio * energy_before)
            predicted = [
                third_in[it, block][0:1, :] + ratio * predicted[block] for block in range(DP)
            ]
            direction_rough = rough + ratio * direction_rough
            predicted_own = message[0:1, :] + ratio * predicted_own
            whole = plane_rows + ratio * whole
        weighted = [setup_in[block, 4:5, :] * predicted[block] for block in range(DP)]
        square = weighted[0] * predicted[0]
        for block in range(1, DP):
            square += weighted[block] * predicted[block]
        step_length = norm_next / (energy + lane_sum(square))
        if it == 0:
            update = step_length * whole
            change = step_length * predicted_own
        else:
            update = update + step_length * whole
            change = change + step_length * predicted_own
        if it < ITERS - 1:
            spread = sens[0] * weighted[0]
            for block in range(1, DP):
                spread += sens[block] * weighted[block]
            image = to_row(spread) + direction_rough
            residual = jnp.where(own, residual - step_length * image, 0.0)
        norm_now = norm_next
        energy_before = energy

    update_out[...] = update
    change_out[...] = change

    await_bytes(setup_in.at[pl.ds(0, DP - 1)], send_sems.at[0])
    await_bytes(static_in, send_sems.at[1])
    await_bytes(field_in.at[pl.ds(0, DP - 1)], field_send)
    for it in range(ITERS):
        sem = 2 + 4 * it
        await_bytes(plane_in.at[it], send_sems.at[sem])
        await_bytes(first_in.at[it, pl.ds(0, DP - 1)], send_sems.at[sem + 1])
        await_bytes(second_in.at[it], send_sems.at[sem + 2])
        await_bytes(third_in.at[it, pl.ds(0, DP - 1)], send_sems.at[sem + 3])


def per_device(configs, pole_fields, misfit, data_weight, conductivity, face_weights):
    vmem = pl.BlockSpec(memory_space=pltpu.VMEM)
    update, change = pl.pallas_call(
        kernel,
        name="inversion",
        out_shape=(
            jax.ShapeDtypeStruct((DP, LANES), F32),
            jax.ShapeDtypeStruct((1, LANES), F32),
        ),
        in_specs=[vmem] * 6,
        out_specs=(vmem, vmem),
        scratch_shapes=[
            pltpu.VMEM((DP, 3 * OWN, POLE_ROWS), BF16),
            pltpu.VMEM((DP, 3 * OWN, POLE_ROWS), BF16),
            pltpu.VMEM((CHUNK, 2 * DATA), BF16),
            pltpu.VMEM((3 * OWN, 2 * DATA), F32),
            pltpu.VMEM((DP, OWN, LANES), F32),
            pltpu.VMEM((8, LANES), F32),
            pltpu.VMEM((DP, 8, LANES), F32),
            pltpu.VMEM((2, LANES), F32),
            pltpu.VMEM((2, 2, LANES), F32),
            pltpu.VMEM((ITERS, DP, 2, LANES), F32),
            pltpu.VMEM((ITERS, DP, 2, LANES), F32),
            pltpu.VMEM((ITERS, 1, LANES), F32),
            pltpu.VMEM((ITERS, 2, 1, LANES), F32),
            pltpu.VMEM((ITERS, 2, LANES), F32),
            pltpu.VMEM((ITERS, CELL - 1, 2, LANES), F32),
            pltpu.VMEM((ITERS, DP, 2, LANES), F32),
            pltpu.SemaphoreType.DMA,
            pltpu.SemaphoreType.DMA((DP,)),
            pltpu.SemaphoreType.DMA((2 + 4 * ITERS,)),
            pltpu.SemaphoreType.DMA((2 + 4 * ITERS,)),
        ],
        compiler_params=pltpu.CompilerParams(
            collective_id=0, has_side_effects=True, vmem_limit_bytes=40 * 1024 * 1024
        ),
    )(
        pole_fields,
        configs.T,
        misfit.reshape(1, LANES),
        data_weight.reshape(1, LANES),
        conductivity.reshape(8, LANES),
        face_weights,
    )
    return update[:, 32:96].reshape(-1), change.reshape(-1)


def solution(mesh):
    placed = (P("dp", None), P(None, "dp", "cell"), P("dp"), P("dp"), P("cell"), P(None, "cell"))
    return jax.shard_map(
        per_device, mesh=mesh, in_specs=placed, out_specs=(P("cell"), P("dp")), check_vma=False
    )
```

```python
import functools
import math

import jax
import jax.numpy as jnp
from jax import lax
from jax.experimental import pallas as pl
from jax.experimental.pallas import tpu as pltpu
from jax.sharding import PartitionSpec as P

GY = 32
GZ = 32
ITERS = 3
DAMPING = 0.2

DP = 16
CELL = 32
OWN = 64
POLE_ROWS = 128
CHUNK = 256
DATA = 2048
LANES = 128
F32 = jnp.float32
BF16 = jnp.bfloat16
MESH = pl.DeviceIdType.MESH


def lane_sum(row):
    return jnp.sum(row, axis=1, keepdims=True)


def kernel(
    fields_hbm,
    configs_hbm,
    misfit_hbm,
    weight_hbm,
    conductivity_hbm,
    faces_hbm,
    update_out,
    change_out,
    fields,
    configs_t,
    misfit,
    weight,
    conductivity,
    faces,
    field_out,
    field_in,
    signs_a,
    signs_b,
    totals,
    sens,
    setup_out,
    setup_in,
    static_out,
    static_in,
    first_out,
    first_in,
    plane_out,
    plane_in,
    second_out,
    second_in,
    third_in,
    field_send,
    field_recv,
    send_sems,
    recv_sems,
    load_sems,
):
    loads = []
    for index, (source, target) in enumerate(
        (
            (fields_hbm, fields),
            (configs_hbm, configs_t),
            (weight_hbm, weight),
            (misfit_hbm, misfit),
            (conductivity_hbm, conductivity),
            (faces_hbm, faces),
        )
    ):
        loads.append(pltpu.make_async_copy(source, target, load_sems.at[index]))
        loads[-1].start()

    dp = lax.axis_index("dp")
    cell = lax.axis_index("cell")
    chip = dp // 2
    core = dp % 2
    above = (cell + 1) % CELL
    below = (cell + CELL - 1) % CELL

    barrier = pltpu.get_barrier_semaphore()
    for step in range(1, DP):
        pl.semaphore_signal(
            barrier, inc=1, device_id={"dp": (dp + step) % DP, "cell": cell}, device_id_type=MESH
        )
    for step in range(1, CELL):
        pl.semaphore_signal(
            barrier, inc=1, device_id={"dp": dp, "cell": (cell + step) % CELL}, device_id_type=MESH
        )

    lane = lax.broadcasted_iota(jnp.int32, (1, LANES), 1)
    own = (lane >= 32) & (lane < 96)

    for load in loads:
        load.wait()

    for target in range(8):
        for part in range(3):
            turned = fields[part, :, target * LANES : (target + 1) * LANES].T
            field_out[2 * target, part * OWN : (part + 1) * OWN, :] = turned[:OWN]
            field_out[2 * target + 1, part * OWN : (part + 1) * OWN, :] = turned[OWN:]
    field_in[dp] = field_out[dp]

    setup_out[0:4, :] = configs_t[...].astype(F32)
    setup_out[4:5, :] = weight[...]
    setup_out[5:6, :] = misfit[...]
    setup_out[6:8, :] = jnp.zeros((2, LANES), F32)
    setup_in[dp] = setup_out[...]

    even = dp % 2 == 0
    tile_a = jnp.maximum((dp + 1) // 2 - 1, 0)
    tile_b = jnp.minimum((dp + 1) // 2, 7)

    def widened(first, second):
        if_even = jnp.where(lane < 32, pltpu.roll(first, 32, 1), pltpu.roll(second, 32, 1))
        if_odd = jnp.where(lane < 96, pltpu.roll(first, 96, 1), pltpu.roll(second, 96, 1))
        return jnp.where(jnp.broadcast_to(even, (1, LANES)), if_even, if_odd)

    def face_row(axis):
        return widened(
            faces[axis : axis + 1, pl.ds(pl.multiple_of(tile_a * LANES, LANES), LANES)],
            faces[axis : axis + 1, pl.ds(pl.multiple_of(tile_b * LANES, LANES), LANES)],
        )

    cond_row = widened(conductivity[pl.ds(tile_a, 1), :], conductivity[pl.ds(tile_b, 1), :])
    face_x, face_y, face_z = face_row(0), face_row(1), face_row(2)
    static_out[0:1, :] = cond_row
    static_out[1:2, :] = face_x

    pl.semaphore_wait(barrier, DP - 1 + CELL - 1)

    def push(source, target, send, recv, to_dp, to_cell):
        pltpu.make_async_remote_copy(
            src_ref=source,
            dst_ref=target,
            send_sem=send,
            recv_sem=recv,
            device_id={"dp": to_dp, "cell": to_cell},
            device_id_type=MESH,
        ).start()

    def await_bytes(ref, sem):
        pltpu.make_async_copy(ref, ref, sem).wait()

    for step in range(1, DP):
        push(setup_out, setup_in.at[dp], send_sems.at[0], recv_sems.at[0], (dp + step) % DP, cell)
    push(static_out, static_in.at[0], send_sems.at[1], recv_sems.at[1], dp, above)
    push(static_out, static_in.at[1], send_sems.at[1], recv_sems.at[1], dp, below)
    for far in (1, 7, 2, 6, 3, 5, 4, 0):
        for other in (0, 1):
            if (far, other) == (0, 0):
                continue
            to = (chip + far) % 8 * 2 + (core + other) % 2
            push(field_out.at[to], field_in.at[dp], field_send, field_recv.at[dp], to, cell)

    await_bytes(setup_in.at[pl.ds(0, DP - 1)], recv_sems.at[0])

    def chunk_of(step):
        half = (step + 1) // 2
        return (chip + (8 - half) % 8 + (step % 2) * (2 * half - 8)) % 8

    def build(signs, step):
        ids = lax.broadcasted_iota(jnp.int32, (CHUNK, 1), 0) + chunk_of(step) * CHUNK
        ids = jnp.broadcast_to(ids.astype(F32), (CHUNK, LANES))
        for block in range(DP):
            for pair in range(2):
                plus = setup_in[block, 2 * pair : 2 * pair + 1, :]
                minus = setup_in[block, 2 * pair + 1 : 2 * pair + 2, :]
                value = jnp.where(ids == plus, 1.0, jnp.where(ids == minus, -1.0, 0.0))
                at = pair * DATA + block * LANES
                signs[:, at : at + LANES] = value.astype(BF16)

    def product(signs, step):
        chunk = chunk_of(step)
        left = jnp.concatenate([field_in[2 * chunk], field_in[2 * chunk + 1]], axis=1)
        return jnp.dot(left, signs[...], preferred_element_type=F32)

    def await_fields(step):
        for part in range(2):
            source = 2 * chunk_of(step) + part
            await_bytes(field_in.at[source], field_recv.at[source])

    build(signs_a, 0)
    sibling = 2 * chip + 1 - core
    await_bytes(field_in.at[sibling], field_recv.at[sibling])
    totals[...] = product(signs_a, 0)
    build(signs_b, 1)

    def two_chunks(turn, carry):
        for signs, later, step in (
            (signs_b, signs_a, 2 * turn + 1),
            (signs_a, signs_b, 2 * turn + 2),
        ):
            await_fields(step)
            totals[...] += product(signs, step)
            build(later, step + 1)
        return carry

    lax.fori_loop(0, 3, two_chunks, 0)
    await_fields(7)
    totals[...] += product(signs_b, 7)

    scale = -1.0 / math.sqrt(DATA)
    gradient_sum = jnp.zeros((OWN, LANES), F32)
    for block in range(DP):
        at, bt = block * LANES, DATA + block * LANES
        value = totals[0:OWN, at : at + LANES] * totals[0:OWN, bt : bt + LANES]
        for part in (1, 2):
            rows = slice(part * OWN, (part + 1) * OWN)
            value += totals[rows, at : at + LANES] * totals[rows, bt : bt + LANES]
        value = value * scale
        sens[block] = value
        gradient_sum += value * (setup_in[block, 4:5, :] * setup_in[block, 5:6, :])

    spot = lax.broadcasted_iota(jnp.int32, (OWN, LANES), 0) + 32 == lax.broadcasted_iota(
        jnp.int32, (OWN, LANES), 1
    )

    def to_row(spread):
        column = jnp.sum(spread, axis=1, keepdims=True)
        return jnp.sum(jnp.where(spot, column, 0.0), axis=0, keepdims=True)

    def to_column(row):
        return jnp.sum(jnp.where(spot, row, 0.0), axis=1, keepdims=True)

    await_bytes(static_in, recv_sems.at[1])

    def masked(row, keep):
        return jnp.where(own & keep, row, 0.0)

    grid_y = 2 * dp + (lane - 32) // 32
    grid_z = lane % 32
    up_x = masked(face_x, jnp.broadcast_to(cell < CELL - 1, (1, LANES)))
    low_x = masked(static_in[0, 1:2, :], jnp.broadcast_to(cell > 0, (1, LANES)))
    up_y = masked(face_y, grid_y < GY - 1)
    low_y = masked(pltpu.roll(face_y, 32, 1), grid_y > 0)
    up_z = masked(face_z, grid_z < GZ - 1)
    low_z = masked(pltpu.roll(face_z, 1, 1), grid_z > 0)

    def roughness(row, lower, upper):
        return (
            up_x * (row - upper)
            + low_x * (row - lower)
            + up_y * (row - pltpu.roll(row, 96, 1))
            + low_y * (row - pltpu.roll(row, 32, 1))
            + up_z * (row - pltpu.roll(row, 127, 1))
            + low_z * (row - pltpu.roll(row, 1, 1))
        )

    residual = to_row(gradient_sum) - roughness(cond_row, static_in[0, 0:1, :], static_in[1, 0:1, :])
    residual = jnp.where(own, residual, 0.0)

    for it in range(ITERS):
        sem = 2 + 4 * it
        column = jnp.broadcast_to(to_column(residual), (OWN, LANES))
        plane_out[it] = residual
        push(plane_out.at[it], plane_in.at[it, 0], send_sems.at[sem], recv_sems.at[sem], dp, above)
        push(plane_out.at[it], plane_in.at[it, 1], send_sems.at[sem], recv_sems.at[sem], dp, below)
        for block in range(DP):
            image_row = jnp.sum(sens[block] * column, axis=0, keepdims=True)
            first_out[it, block] = jnp.concatenate([image_row, residual], axis=0)
        for step in (8, 7, 9, 6, 10, 5, 11, 4, 12, 3, 13, 2, 14, 1, 15):
            to = (dp + step) % DP
            push(
                first_out.at[it, to],
                first_in.at[it, dp],
                send_sems.at[sem + 1],
                recv_sems.at[sem + 1],
                to,
                cell,
            )
        first_in[it, dp] = first_out[it, dp]
        await_bytes(plane_in.at[it], recv_sems.at[sem])
        await_bytes(first_in.at[it, pl.ds(0, DP - 1)], recv_sems.at[sem + 1])
        gathered = first_in[it]
        partial = jnp.sum(gathered[:, 0:1, :], axis=0)
        before = first_in[it, (dp + DP - 1) % DP][1:2, :]
        after = first_in[it, (dp + 1) % DP][1:2, :]
        wide = jnp.where(
            own, residual, pltpu.roll(jnp.where(lane >= 64, before, after), 64, 1)
        )
        rough = roughness(wide, plane_in[it, 0], plane_in[it, 1]) + DAMPING * residual
        scalars = jnp.where(lane == 0, lane_sum(residual * residual), 0.0)
        scalars = jnp.where(lane == 1, lane_sum(residual * rough), scalars)
        if it > 0:
            scalars = jnp.where(lane == 2, lane_sum(residual * direction_rough), scalars)
        message = jnp.concatenate([partial, scalars], axis=0)
        second_out[it] = message
        for step in range(1, CELL):
            push(
                second_out.at[it],
                second_in.at[it, step - 1],
                send_sems.at[sem + 2],
                recv_sems.at[sem + 2],
                dp,
                (cell + step) % CELL,
            )
        await_bytes(second_in.at[it], recv_sems.at[sem + 2])
        message = message + jnp.sum(second_in[it], axis=0)
        third_in[it, dp] = message
        for step in (8, 7, 9, 6, 10, 5, 11, 4, 12, 3, 13, 2, 14, 1, 15):
            push(
                third_in.at[it, dp],
                third_in.at[it, dp],
                send_sems.at[sem + 3],
                recv_sems.at[sem + 3],
                (dp + step) % DP,
                cell,
            )
        await_bytes(third_in.at[it, pl.ds(0, DP - 1)], recv_sems.at[sem + 3])
        sums = jnp.sum(third_in[it][:, 1:2, :], axis=0)
        norm_next = sums[:, 0:1]
        energy = sums[:, 1:2]
        plane_rows = gathered[:, 1, :]
        if it == 0:
            predicted = [third_in[it, block][0:1, :] for block in range(DP)]
            direction_rough = rough
            predicted_own = message[0:1, :]
            whole = plane_rows
        else:
            ratio = norm_next / norm_now
            energy = energy + ratio * (2.0 * sums[:, 2:3] + ratio * energy_before)
            predicted = [
                third_in[it, block][0:1, :] + ratio * predicted[block] for block in range(DP)
            ]
            direction_rough = rough + ratio * direction_rough
            predicted_own = message[0:1, :] + ratio * predicted_own
            whole = plane_rows + ratio * whole
        weighted = [setup_in[block, 4:5, :] * predicted[block] for block in range(DP)]
        square = weighted[0] * predicted[0]
        for block in range(1, DP):
            square += weighted[block] * predicted[block]
        step_length = norm_next / (energy + lane_sum(square))
        if it == 0:
            update = step_length * whole
            change = step_length * predicted_own
        else:
            update = update + step_length * whole
            change = change + step_length * predicted_own
        if it < ITERS - 1:
            spread = sens[0] * weighted[0]
            for block in range(1, DP):
                spread += sens[block] * weighted[block]
            image = to_row(spread) + direction_rough
            residual = jnp.where(own, residual - step_length * image, 0.0)
        norm_now = norm_next
        energy_before = energy

    update_out[...] = update
    change_out[...] = change

    await_bytes(setup_in.at[pl.ds(0, DP - 1)], send_sems.at[0])
    await_bytes(static_in, send_sems.at[1])
    await_bytes(field_in.at[pl.ds(0, DP - 1)], field_send)
    for it in range(ITERS):
        sem = 2 + 4 * it
        await_bytes(plane_in.at[it], send_sems.at[sem])
        await_bytes(first_in.at[it, pl.ds(0, DP - 1)], send_sems.at[sem + 1])
        await_bytes(second_in.at[it], send_sems.at[sem + 2])
        await_bytes(third_in.at[it, pl.ds(0, DP - 1)], send_sems.at[sem + 3])


def per_device(configs, pole_fields, misfit, data_weight, conductivity, face_weights):
    vmem = pl.BlockSpec(memory_space=pltpu.VMEM)
    update, change = pl.pallas_call(
        kernel,
        name="inversion",
        out_shape=(
            jax.ShapeDtypeStruct((DP, LANES), F32),
            jax.ShapeDtypeStruct((1, LANES), F32),
        ),
        in_specs=[pl.BlockSpec(memory_space=pltpu.HBM)] * 6,
        out_specs=(vmem, vmem),
        scratch_shapes=[
            pltpu.VMEM((3, POLE_ROWS, 8 * LANES), BF16),
            pltpu.VMEM((4, LANES), jnp.int32),
            pltpu.VMEM((1, LANES), F32),
            pltpu.VMEM((1, LANES), F32),
            pltpu.VMEM((8, LANES), F32),
            pltpu.VMEM((3, 8 * LANES), F32),
            pltpu.VMEM((DP, 3 * OWN, POLE_ROWS), BF16),
            pltpu.VMEM((DP, 3 * OWN, POLE_ROWS), BF16),
            pltpu.VMEM((CHUNK, 2 * DATA), BF16),
            pltpu.VMEM((CHUNK, 2 * DATA), BF16),
            pltpu.VMEM((3 * OWN, 2 * DATA), F32),
            pltpu.VMEM((DP, OWN, LANES), F32),
            pltpu.VMEM((8, LANES), F32),
            pltpu.VMEM((DP, 8, LANES), F32),
            pltpu.VMEM((2, LANES), F32),
            pltpu.VMEM((2, 2, LANES), F32),
            pltpu.VMEM((ITERS, DP, 2, LANES), F32),
            pltpu.VMEM((ITERS, DP, 2, LANES), F32),
            pltpu.VMEM((ITERS, 1, LANES), F32),
            pltpu.VMEM((ITERS, 2, 1, LANES), F32),
            pltpu.VMEM((ITERS, 2, LANES), F32),
            pltpu.VMEM((ITERS, CELL - 1, 2, LANES), F32),
            pltpu.VMEM((ITERS, DP, 2, LANES), F32),
            pltpu.SemaphoreType.DMA,
            pltpu.SemaphoreType.DMA((DP,)),
            pltpu.SemaphoreType.DMA((2 + 4 * ITERS,)),
            pltpu.SemaphoreType.DMA((2 + 4 * ITERS,)),
            pltpu.SemaphoreType.DMA((6,)),
        ],
        compiler_params=pltpu.CompilerParams(
            collective_id=0, has_side_effects=True, vmem_limit_bytes=40 * 1024 * 1024
        ),
    )(
        pole_fields,
        configs.T,
        misfit.reshape(1, LANES),
        data_weight.reshape(1, LANES),
        conductivity.reshape(8, LANES),
        face_weights,
    )
    return update[:, 32:96].reshape(-1), change.reshape(-1)


def solution(mesh):
    placed = (P("dp", None), P(None, "dp", "cell"), P("dp"), P("dp"), P("cell"), P(None, "cell"))
    return jax.shard_map(
        per_device, mesh=mesh, in_specs=placed, out_specs=(P("cell"), P("dp")), check_vma=False
    )
```

```python
import functools
import math

import jax
import jax.numpy as jnp
from jax import lax
from jax.experimental import pallas as pl
from jax.experimental.pallas import tpu as pltpu
from jax.sharding import PartitionSpec as P

GY = 32
GZ = 32
ITERS = 3
DAMPING = 0.2

DP = 16
CELL = 32
OWN = 64
POLE_ROWS = 128
CHUNK = 256
DATA = 2048
LANES = 128
F32 = jnp.float32
BF16 = jnp.bfloat16
MESH = pl.DeviceIdType.MESH

FAR = (4, 3, 5, 2, 6, 1, 7, 0)
PLANE = [(c, x, y) for x in (2, 1, 3, 0) for y in FAR for c in (0, 1) if (c, x, y) != (0, 0, 0)]
COLUMN = [(z, c, y) for z in FAR for y in (1, 0) for c in (0, 1) if (z, c, y) != (0, 0, 0)]


def lane_sum(row):
    return jnp.sum(row, axis=1, keepdims=True)


def kernel(
    fields_hbm,
    configs_hbm,
    misfit_hbm,
    weight_hbm,
    conductivity_hbm,
    faces_hbm,
    update_out,
    change_out,
    fields,
    configs_t,
    misfit,
    weight,
    conductivity,
    faces,
    field_out,
    field_in,
    signs_a,
    signs_b,
    totals,
    sens,
    setup_out,
    setup_in,
    static_out,
    static_in,
    halo_out,
    halo_in,
    first_out,
    first_in,
    second_in,
    scalar_out,
    scalar_in,
    field_send,
    field_recv,
    send_sems,
    recv_sems,
    load_sems,
):
    loads = []
    for index, (source, target) in enumerate(
        (
            (fields_hbm, fields),
            (configs_hbm, configs_t),
            (weight_hbm, weight),
            (misfit_hbm, misfit),
            (conductivity_hbm, conductivity),
            (faces_hbm, faces),
        )
    ):
        loads.append(pltpu.make_async_copy(source, target, load_sems.at[index]))
        loads[-1].start()

    dp = lax.axis_index("dp")
    cell = lax.axis_index("cell")
    chip = dp // 2
    core = dp % 2
    above = (cell + 1) % CELL
    below = (cell + CELL - 1) % CELL

    barrier = pltpu.get_barrier_semaphore()
    for to_core, to_x, to_y in PLANE:
        pl.semaphore_signal(
            barrier,
            inc=1,
            device_id={
                "dp": 2 * chip + (core + to_core) % 2,
                "cell": (cell // 8 + to_x) % 4 * 8 + (cell + to_y) % 8,
            },
            device_id_type=MESH,
        )
    for to_z, to_core, to_pair in COLUMN:
        if to_z != 0:
            pl.semaphore_signal(
                barrier,
                inc=1,
                device_id={
                    "dp": (chip + to_z) % 8 * 2 + (core + to_core) % 2,
                    "cell": cell + to_pair * (1 - 2 * (cell % 2)),
                },
                device_id_type=MESH,
            )

    lane = lax.broadcasted_iota(jnp.int32, (1, LANES), 1)
    own = (lane >= 32) & (lane < 96)

    for load in loads:
        load.wait()

    for target in range(8):
        for part in range(3):
            turned = fields[part, :, target * LANES : (target + 1) * LANES].T
            field_out[2 * target, part * OWN : (part + 1) * OWN, :] = turned[:OWN]
            field_out[2 * target + 1, part * OWN : (part + 1) * OWN, :] = turned[OWN:]
    field_in[dp] = field_out[dp]

    setup_out[0:4, :] = configs_t[...].astype(F32)
    setup_out[4:5, :] = weight[...]
    setup_out[5:6, :] = misfit[...]
    setup_out[6:8, :] = jnp.zeros((2, LANES), F32)
    setup_in[dp] = setup_out[...]

    even = dp % 2 == 0
    tile_a = jnp.maximum((dp + 1) // 2 - 1, 0)
    tile_b = jnp.minimum((dp + 1) // 2, 7)

    def widened(first, second):
        if_even = jnp.where(lane < 32, pltpu.roll(first, 32, 1), pltpu.roll(second, 32, 1))
        if_odd = jnp.where(lane < 96, pltpu.roll(first, 96, 1), pltpu.roll(second, 96, 1))
        return jnp.where(jnp.broadcast_to(even, (1, LANES)), if_even, if_odd)

    def face_row(axis):
        return widened(
            faces[axis : axis + 1, pl.ds(pl.multiple_of(tile_a * LANES, LANES), LANES)],
            faces[axis : axis + 1, pl.ds(pl.multiple_of(tile_b * LANES, LANES), LANES)],
        )

    cond_row = widened(conductivity[pl.ds(tile_a, 1), :], conductivity[pl.ds(tile_b, 1), :])
    face_x, face_y, face_z = face_row(0), face_row(1), face_row(2)
    static_out[0:1, :] = cond_row
    static_out[1:2, :] = face_x

    pl.semaphore_wait(barrier, 63 + 28)

    def push(source, target, send, recv, to_dp, to_cell):
        pltpu.make_async_remote_copy(
            src_ref=source,
            dst_ref=target,
            send_sem=send,
            recv_sem=recv,
            device_id={"dp": to_dp, "cell": to_cell},
            device_id_type=MESH,
        ).start()

    def await_bytes(ref, sem):
        pltpu.make_async_copy(ref, ref, sem).wait()

    for step in range(1, DP):
        push(setup_out, setup_in.at[dp], send_sems.at[0], recv_sems.at[0], (dp + step) % DP, cell)
    push(static_out, static_in.at[0], send_sems.at[1], recv_sems.at[1], dp, above)
    push(static_out, static_in.at[1], send_sems.at[1], recv_sems.at[1], dp, below)
    for far in (1, 7, 2, 6, 3, 5, 4, 0):
        for other in (0, 1):
            if (far, other) == (0, 0):
                continue
            to = (chip + far) % 8 * 2 + (core + other) % 2
            push(field_out.at[to], field_in.at[dp], field_send, field_recv.at[dp], to, cell)

    await_bytes(setup_in.at[pl.ds(0, DP - 1)], recv_sems.at[0])

    def chunk_of(step):
        half = (step + 1) // 2
        return (chip + (8 - half) % 8 + (step % 2) * (2 * half - 8)) % 8

    def build(signs, step):
        ids = lax.broadcasted_iota(jnp.int32, (CHUNK, 1), 0) + chunk_of(step) * CHUNK
        ids = jnp.broadcast_to(ids.astype(F32), (CHUNK, LANES))
        for block in range(DP):
            for pair in range(2):
                plus = setup_in[block, 2 * pair : 2 * pair + 1, :]
                minus = setup_in[block, 2 * pair + 1 : 2 * pair + 2, :]
                value = jnp.where(ids == plus, 1.0, jnp.where(ids == minus, -1.0, 0.0))
                at = pair * DATA + block * LANES
                signs[:, at : at + LANES] = value.astype(BF16)

    def product(signs, step):
        chunk = chunk_of(step)
        left = jnp.concatenate([field_in[2 * chunk], field_in[2 * chunk + 1]], axis=1)
        return jnp.dot(left, signs[...], preferred_element_type=F32)

    def await_fields(step):
        for part in range(2):
            source = 2 * chunk_of(step) + part
            await_bytes(field_in.at[source], field_recv.at[source])

    build(signs_a, 0)
    sibling = 2 * chip + 1 - core
    await_bytes(field_in.at[sibling], field_recv.at[sibling])
    totals[...] = product(signs_a, 0)
    build(signs_b, 1)

    def two_chunks(turn, carry):
        for signs, later, step in (
            (signs_b, signs_a, 2 * turn + 1),
            (signs_a, signs_b, 2 * turn + 2),
        ):
            await_fields(step)
            totals[...] += product(signs, step)
            build(later, step + 1)
        return carry

    lax.fori_loop(0, 3, two_chunks, 0)
    await_fields(7)
    totals[...] += product(signs_b, 7)

    scale = -1.0 / math.sqrt(DATA)
    gradient_sum = jnp.zeros((OWN, LANES), F32)
    for block in range(DP):
        at, bt = block * LANES, DATA + block * LANES
        value = totals[0:OWN, at : at + LANES] * totals[0:OWN, bt : bt + LANES]
        for part in (1, 2):
            rows = slice(part * OWN, (part + 1) * OWN)
            value += totals[rows, at : at + LANES] * totals[rows, bt : bt + LANES]
        value = value * scale
        sens[block] = value
        gradient_sum += value * (setup_in[block, 4:5, :] * setup_in[block, 5:6, :])

    spot = lax.broadcasted_iota(jnp.int32, (OWN, LANES), 0) + 32 == lax.broadcasted_iota(
        jnp.int32, (OWN, LANES), 1
    )

    def to_row(spread):
        column = jnp.sum(spread, axis=1, keepdims=True)
        return jnp.sum(jnp.where(spot, column, 0.0), axis=0, keepdims=True)

    def to_column(row):
        return jnp.sum(jnp.where(spot, row, 0.0), axis=1, keepdims=True)

    await_bytes(static_in, recv_sems.at[1])

    def masked(row, keep):
        return jnp.where(own & keep, row, 0.0)

    grid_y = 2 * dp + (lane - 32) // 32
    grid_z = lane % 32
    up_x = masked(face_x, jnp.broadcast_to(cell < CELL - 1, (1, LANES)))
    low_x = masked(static_in[0, 1:2, :], jnp.broadcast_to(cell > 0, (1, LANES)))
    up_y = masked(face_y, grid_y < GY - 1)
    low_y = masked(pltpu.roll(face_y, 32, 1), grid_y > 0)
    up_z = masked(face_z, grid_z < GZ - 1)
    low_z = masked(pltpu.roll(face_z, 1, 1), grid_z > 0)

    def roughness(row, lower, upper):
        return (
            up_x * (row - upper)
            + low_x * (row - lower)
            + up_y * (row - pltpu.roll(row, 96, 1))
            + low_y * (row - pltpu.roll(row, 32, 1))
            + up_z * (row - pltpu.roll(row, 127, 1))
            + low_z * (row - pltpu.roll(row, 1, 1))
        )

    residual = to_row(gradient_sum) - roughness(cond_row, static_in[0, 0:1, :], static_in[1, 0:1, :])
    residual = jnp.where(own, residual, 0.0)

    quarter = core + 2 * (cell % 2)
    for it in range(ITERS):
        sem = 2 + 5 * it
        halo_out[it] = residual
        for slot, (to_dp, to_cell) in enumerate(
            (
                (dp, above),
                (dp, below),
                ((dp + 1) % DP, cell),
                ((dp + DP - 1) % DP, cell),
            )
        ):
            push(
                halo_out.at[it],
                halo_in.at[it, slot],
                send_sems.at[sem],
                recv_sems.at[sem],
                to_dp,
                to_cell,
            )
        column = jnp.broadcast_to(to_column(residual), (OWN, LANES))
        for part in range(4):
            first_out[it, part] = jnp.concatenate(
                [
                    jnp.sum(sens[4 * part + row] * column, axis=0, keepdims=True)
                    for row in range(4)
                ],
                axis=0,
            )
        for slot, (to_core, to_x, to_y) in enumerate(PLANE):
            to_dp = 2 * chip + (core + to_core) % 2
            to_cell = (cell // 8 + to_x) % 4 * 8 + (cell + to_y) % 8
            push(
                first_out.at[it, to_dp % 2 + 2 * (to_cell % 2)],
                first_in.at[it, slot],
                send_sems.at[sem + 1],
                recv_sems.at[sem + 1],
                to_dp,
                to_cell,
            )

        await_bytes(halo_in.at[it], recv_sems.at[sem])
        before, after = halo_in[it, 2], halo_in[it, 3]
        wide = jnp.where(own, residual, pltpu.roll(jnp.where(lane >= 64, before, after), 64, 1))
        rough = roughness(wide, halo_in[it, 0], halo_in[it, 1]) + DAMPING * residual
        scalars = jnp.where(lane == 0, lane_sum(residual * residual), 0.0)
        scalars = jnp.where(lane == 1, lane_sum(residual * rough), scalars)
        if it > 0:
            scalars = jnp.where(lane == 2, lane_sum(residual * direction_rough), scalars)
        scalar_out[it, 0] = scalars
        for slot, (to_core, to_x, to_y) in enumerate(PLANE):
            push(
                scalar_out.at[it, 0],
                scalar_in.at[it, slot],
                send_sems.at[sem + 3],
                recv_sems.at[sem + 3],
                2 * chip + (core + to_core) % 2,
                (cell // 8 + to_x) % 4 * 8 + (cell + to_y) % 8,
            )

        await_bytes(first_in.at[it], recv_sems.at[sem + 1])
        partial = first_out[it, quarter] + jnp.sum(first_in[it], axis=0)
        second_in[it, 4 * chip + quarter] = jnp.concatenate([partial, residual], axis=0)
        for to_z, to_core, to_pair in COLUMN:
            push(
                second_in.at[it, 4 * chip + quarter],
                second_in.at[it, 4 * chip + quarter],
                send_sems.at[sem + 2],
                recv_sems.at[sem + 2],
                (chip + to_z) % 8 * 2 + (core + to_core) % 2,
                cell + to_pair * (1 - 2 * (cell % 2)),
            )

        await_bytes(scalar_in.at[it, pl.ds(0, 63)], recv_sems.at[sem + 3])
        scalars = scalars + jnp.sum(scalar_in[it, 0:63], axis=0)
        scalar_out[it, 1] = scalars
        for slot, to_z in enumerate((4, 3, 5, 2, 6, 1, 7)):
            push(
                scalar_out.at[it, 1],
                scalar_in.at[it, 63 + slot],
                send_sems.at[sem + 4],
                recv_sems.at[sem + 4],
                (chip + to_z) % 8 * 2 + core,
                cell,
            )

        await_bytes(second_in.at[it, pl.ds(0, 31)], recv_sems.at[sem + 2])
        quarters = [second_in[it, part] for part in range(4)]
        for plane in range(1, 8):
            for part in range(4):
                quarters[part] += second_in[it, 4 * plane + part]
        rows = [quarters[block // 4][block % 4 : block % 4 + 1] for block in range(DP)]
        await_bytes(scalar_in.at[it, pl.ds(63, 7)], recv_sems.at[sem + 4])
        sums = scalars + jnp.sum(scalar_in[it, 63:70], axis=0)
        norm_next = sums[:, 0:1]
        energy = sums[:, 1:2]
        plane_rows = jnp.concatenate(
            [
                second_in[it, source // 2 * 4 + source % 2 + 2 * (cell % 2)][4:5]
                for source in range(DP)
            ],
            axis=0,
        )
        if it == 0:
            predicted = rows
            direction_rough = rough
            whole = plane_rows
        else:
            ratio = norm_next / norm_now
            energy = energy + ratio * (2.0 * sums[:, 2:3] + ratio * energy_before)
            predicted = [rows[block] + ratio * predicted[block] for block in range(DP)]
            direction_rough = rough + ratio * direction_rough
            whole = plane_rows + ratio * whole
        weighted = [setup_in[block, 4:5, :] * predicted[block] for block in range(DP)]
        square = weighted[0] * predicted[0]
        for block in range(1, DP):
            square += weighted[block] * predicted[block]
        step_length = norm_next / (energy + lane_sum(square))
        if it < ITERS - 1:
            spread = sens[0] * weighted[0]
            for block in range(1, DP):
                spread += sens[block] * weighted[block]
            image = to_row(spread) + direction_rough
            residual = jnp.where(own, residual - step_length * image, 0.0)
        predicted_rows = jnp.concatenate(predicted, axis=0)
        if it == 0:
            update = step_length * whole
            change = step_length * predicted_rows
        else:
            update = update + step_length * whole
            change = change + step_length * predicted_rows
        norm_now = norm_next
        energy_before = energy

    update_out[...] = update
    mine = lax.broadcasted_iota(jnp.int32, (DP, LANES), 0) == dp
    change_out[...] = jnp.sum(jnp.where(mine, change, 0.0), axis=0, keepdims=True)

    await_bytes(setup_in.at[pl.ds(0, DP - 1)], send_sems.at[0])
    await_bytes(static_in, send_sems.at[1])
    await_bytes(field_in.at[pl.ds(0, DP - 1)], field_send)
    for it in range(ITERS):
        sem = 2 + 5 * it
        await_bytes(halo_in.at[it], send_sems.at[sem])
        await_bytes(first_in.at[it], send_sems.at[sem + 1])
        await_bytes(second_in.at[it, pl.ds(0, 31)], send_sems.at[sem + 2])
        await_bytes(scalar_in.at[it, pl.ds(0, 63)], send_sems.at[sem + 3])
        await_bytes(scalar_in.at[it, pl.ds(63, 7)], send_sems.at[sem + 4])


def per_device(configs, pole_fields, misfit, data_weight, conductivity, face_weights):
    vmem = pl.BlockSpec(memory_space=pltpu.VMEM)
    update, change = pl.pallas_call(
        kernel,
        name="inversion",
        out_shape=(
            jax.ShapeDtypeStruct((DP, LANES), F32),
            jax.ShapeDtypeStruct((1, LANES), F32),
        ),
        in_specs=[pl.BlockSpec(memory_space=pltpu.HBM)] * 6,
        out_specs=(vmem, vmem),
        scratch_shapes=[
            pltpu.VMEM((3, POLE_ROWS, 8 * LANES), BF16),
            pltpu.VMEM((4, LANES), jnp.int32),
            pltpu.VMEM((1, LANES), F32),
            pltpu.VMEM((1, LANES), F32),
            pltpu.VMEM((8, LANES), F32),
            pltpu.VMEM((3, 8 * LANES), F32),
            pltpu.VMEM((DP, 3 * OWN, POLE_ROWS), BF16),
            pltpu.VMEM((DP, 3 * OWN, POLE_ROWS), BF16),
            pltpu.VMEM((CHUNK, 2 * DATA), BF16),
            pltpu.VMEM((CHUNK, 2 * DATA), BF16),
            pltpu.VMEM((3 * OWN, 2 * DATA), F32),
            pltpu.VMEM((DP, OWN, LANES), F32),
            pltpu.VMEM((8, LANES), F32),
            pltpu.VMEM((DP, 8, LANES), F32),
            pltpu.VMEM((2, LANES), F32),
            pltpu.VMEM((2, 2, LANES), F32),
            pltpu.VMEM((ITERS, 1, LANES), F32),
            pltpu.VMEM((ITERS, 4, 1, LANES), F32),
            pltpu.VMEM((ITERS, 4, 4, LANES), F32),
            pltpu.VMEM((ITERS, 63, 4, LANES), F32),
            pltpu.VMEM((ITERS, 32, 5, LANES), F32),
            pltpu.VMEM((ITERS, 2, 1, LANES), F32),
            pltpu.VMEM((ITERS, 70, 1, LANES), F32),
            pltpu.SemaphoreType.DMA,
            pltpu.SemaphoreType.DMA((DP,)),
            pltpu.SemaphoreType.DMA((2 + 5 * ITERS,)),
            pltpu.SemaphoreType.DMA((2 + 5 * ITERS,)),
            pltpu.SemaphoreType.DMA((6,)),
        ],
        compiler_params=pltpu.CompilerParams(
            collective_id=0, has_side_effects=True, vmem_limit_bytes=40 * 1024 * 1024
        ),
    )(
        pole_fields,
        configs.T,
        misfit.reshape(1, LANES),
        data_weight.reshape(1, LANES),
        conductivity.reshape(8, LANES),
        face_weights,
    )
    return update[:, 32:96].reshape(-1), change.reshape(-1)


def solution(mesh):
    placed = (P("dp", None), P(None, "dp", "cell"), P("dp"), P("dp"), P("cell"), P(None, "cell"))
    return jax.shard_map(
        per_device, mesh=mesh, in_specs=placed, out_specs=(P("cell"), P("dp")), check_vma=False
    )
```

```python
import functools
import math

import jax
import jax.numpy as jnp
from jax import lax
from jax.experimental import pallas as pl
from jax.experimental.pallas import tpu as pltpu
from jax.sharding import PartitionSpec as P

GY = 32
GZ = 32
ITERS = 3
DAMPING = 0.2

DP = 16
CELL = 32
OWN = 64
POLE_ROWS = 128
CHUNK = 256
DATA = 2048
LANES = 128
F32 = jnp.float32
BF16 = jnp.bfloat16
MESH = pl.DeviceIdType.MESH

FAR = (4, 3, 5, 2, 6, 1, 7, 0)
PLANE = [(c, x, y) for x in (2, 1, 3, 0) for y in FAR for c in (0, 1) if (c, x, y) != (0, 0, 0)]
COLUMN = [(z, c, y) for z in FAR for y in (1, 0) for c in (0, 1) if (z, c, y) != (0, 0, 0)]


def lane_sum(row):
    return jnp.sum(row, axis=1, keepdims=True)


def kernel(
    fields_hbm,
    configs_hbm,
    misfit_hbm,
    weight_hbm,
    conductivity_hbm,
    faces_hbm,
    update_out,
    change_out,
    fields,
    configs_t,
    misfit,
    weight,
    conductivity,
    faces,
    field_out,
    field_in,
    signs_a,
    signs_b,
    totals,
    sens,
    setup_out,
    setup_in,
    static_out,
    static_in,
    halo_out,
    halo_in,
    first_out,
    first_in,
    second_in,
    scalar_out,
    scalar_in,
    field_send,
    field_recv,
    send_sems,
    recv_sems,
    load_sems,
):
    loads = []
    for index, (source, target) in enumerate(
        (
            (fields_hbm, fields),
            (configs_hbm, configs_t),
            (weight_hbm, weight),
            (misfit_hbm, misfit),
            (conductivity_hbm, conductivity),
            (faces_hbm, faces),
        )
    ):
        loads.append(pltpu.make_async_copy(source, target, load_sems.at[index]))
        loads[-1].start()

    dp = lax.axis_index("dp")
    cell = lax.axis_index("cell")
    chip = dp // 2
    core = dp % 2
    above = (cell + 1) % CELL
    below = (cell + CELL - 1) % CELL

    barrier = pltpu.get_barrier_semaphore()
    for to_core, to_x, to_y in PLANE:
        pl.semaphore_signal(
            barrier,
            inc=1,
            device_id={
                "dp": 2 * chip + (core + to_core) % 2,
                "cell": (cell // 8 + to_x) % 4 * 8 + (cell + to_y) % 8,
            },
            device_id_type=MESH,
        )
    for to_z, to_core, to_pair in COLUMN:
        if to_z != 0:
            pl.semaphore_signal(
                barrier,
                inc=1,
                device_id={
                    "dp": (chip + to_z) % 8 * 2 + (core + to_core) % 2,
                    "cell": cell + to_pair * (1 - 2 * (cell % 2)),
                },
                device_id_type=MESH,
            )

    lane = lax.broadcasted_iota(jnp.int32, (1, LANES), 1)
    own = (lane >= 32) & (lane < 96)

    for load in loads:
        load.wait()

    for target in range(8):
        for part in range(3):
            turned = fields[part, :, target * LANES : (target + 1) * LANES].T
            field_out[2 * target, part * OWN : (part + 1) * OWN, :] = turned[:OWN]
            field_out[2 * target + 1, part * OWN : (part + 1) * OWN, :] = turned[OWN:]
    field_in[dp] = field_out[dp]

    setup_out[0:4, :] = configs_t[...].astype(F32)
    setup_out[4:5, :] = weight[...]
    setup_out[5:6, :] = misfit[...]
    setup_out[6:8, :] = jnp.zeros((2, LANES), F32)
    setup_in[dp] = setup_out[...]

    even = dp % 2 == 0
    tile_a = jnp.maximum((dp + 1) // 2 - 1, 0)
    tile_b = jnp.minimum((dp + 1) // 2, 7)

    def widened(first, second):
        if_even = jnp.where(lane < 32, pltpu.roll(first, 32, 1), pltpu.roll(second, 32, 1))
        if_odd = jnp.where(lane < 96, pltpu.roll(first, 96, 1), pltpu.roll(second, 96, 1))
        return jnp.where(jnp.broadcast_to(even, (1, LANES)), if_even, if_odd)

    def face_row(axis):
        return widened(
            faces[axis : axis + 1, pl.ds(pl.multiple_of(tile_a * LANES, LANES), LANES)],
            faces[axis : axis + 1, pl.ds(pl.multiple_of(tile_b * LANES, LANES), LANES)],
        )

    cond_row = widened(conductivity[pl.ds(tile_a, 1), :], conductivity[pl.ds(tile_b, 1), :])
    face_x, face_y, face_z = face_row(0), face_row(1), face_row(2)
    static_out[0:1, :] = cond_row
    static_out[1:2, :] = face_x

    pl.semaphore_wait(barrier, 63 + 28)

    def push(source, target, send, recv, to_dp, to_cell):
        pltpu.make_async_remote_copy(
            src_ref=source,
            dst_ref=target,
            send_sem=send,
            recv_sem=recv,
            device_id={"dp": to_dp, "cell": to_cell},
            device_id_type=MESH,
        ).start()

    def await_bytes(ref, sem):
        pltpu.make_async_copy(ref, ref, sem).wait()

    for step in range(1, DP):
        push(setup_out, setup_in.at[dp], send_sems.at[0], recv_sems.at[0], (dp + step) % DP, cell)
    push(static_out, static_in.at[0], send_sems.at[1], recv_sems.at[1], dp, above)
    push(static_out, static_in.at[1], send_sems.at[1], recv_sems.at[1], dp, below)
    for far in (1, 7, 2, 6, 3, 5, 4, 0):
        for other in (0, 1):
            if (far, other) == (0, 0):
                continue
            to = (chip + far) % 8 * 2 + (core + other) % 2
            push(field_out.at[to], field_in.at[dp], field_send, field_recv.at[dp], to, cell)

    await_bytes(setup_in.at[pl.ds(0, DP - 1)], recv_sems.at[0])

    def chunk_of(step):
        half = (step + 1) // 2
        return (chip + (8 - half) % 8 + (step % 2) * (2 * half - 8)) % 8

    def build(signs, step):
        ids = lax.broadcasted_iota(jnp.int32, (CHUNK, 1), 0) + chunk_of(step) * CHUNK
        ids = jnp.broadcast_to(ids.astype(F32), (CHUNK, LANES))
        for block in range(DP):
            for pair in range(2):
                plus = setup_in[block, 2 * pair : 2 * pair + 1, :]
                minus = setup_in[block, 2 * pair + 1 : 2 * pair + 2, :]
                value = jnp.where(ids == plus, 1.0, jnp.where(ids == minus, -1.0, 0.0))
                at = pair * DATA + block * LANES
                signs[:, at : at + LANES] = value.astype(BF16)

    def product(signs, step):
        chunk = chunk_of(step)
        left = jnp.concatenate([field_in[2 * chunk], field_in[2 * chunk + 1]], axis=1)
        return jnp.dot(left, signs[...], preferred_element_type=F32)

    def await_fields(step):
        for part in range(2):
            source = 2 * chunk_of(step) + part
            await_bytes(field_in.at[source], field_recv.at[source])

    build(signs_a, 0)
    sibling = 2 * chip + 1 - core
    await_bytes(field_in.at[sibling], field_recv.at[sibling])
    totals[...] = product(signs_a, 0)
    build(signs_b, 1)

    def two_chunks(turn, carry):
        for signs, later, step in (
            (signs_b, signs_a, 2 * turn + 1),
            (signs_a, signs_b, 2 * turn + 2),
        ):
            await_fields(step)
            totals[...] += product(signs, step)
            build(later, step + 1)
        return carry

    lax.fori_loop(0, 3, two_chunks, 0)
    await_fields(7)
    totals[...] += product(signs_b, 7)

    scale = -1.0 / math.sqrt(DATA)
    gradient_sum = jnp.zeros((OWN, LANES), F32)
    for block in range(DP):
        at, bt = block * LANES, DATA + block * LANES
        value = totals[0:OWN, at : at + LANES] * totals[0:OWN, bt : bt + LANES]
        for part in (1, 2):
            rows = slice(part * OWN, (part + 1) * OWN)
            value += totals[rows, at : at + LANES] * totals[rows, bt : bt + LANES]
        value = value * scale
        sens[block] = value
        gradient_sum += value * (setup_in[block, 4:5, :] * setup_in[block, 5:6, :])

    spot = lax.broadcasted_iota(jnp.int32, (OWN, LANES), 0) + 32 == lax.broadcasted_iota(
        jnp.int32, (OWN, LANES), 1
    )

    def to_row(spread):
        column = jnp.sum(spread, axis=1, keepdims=True)
        return jnp.sum(jnp.where(spot, column, 0.0), axis=0, keepdims=True)

    def to_column(row):
        return jnp.sum(jnp.where(spot, row, 0.0), axis=1, keepdims=True)

    await_bytes(static_in, recv_sems.at[1])

    def masked(row, keep):
        return jnp.where(own & keep, row, 0.0)

    grid_y = 2 * dp + (lane - 32) // 32
    grid_z = lane % 32
    up_x = masked(face_x, jnp.broadcast_to(cell < CELL - 1, (1, LANES)))
    low_x = masked(static_in[0, 1:2, :], jnp.broadcast_to(cell > 0, (1, LANES)))
    up_y = masked(face_y, grid_y < GY - 1)
    low_y = masked(pltpu.roll(face_y, 32, 1), grid_y > 0)
    up_z = masked(face_z, grid_z < GZ - 1)
    low_z = masked(pltpu.roll(face_z, 1, 1), grid_z > 0)

    def roughness(row, lower, upper):
        return (
            up_x * (row - upper)
            + low_x * (row - lower)
            + up_y * (row - pltpu.roll(row, 96, 1))
            + low_y * (row - pltpu.roll(row, 32, 1))
            + up_z * (row - pltpu.roll(row, 127, 1))
            + low_z * (row - pltpu.roll(row, 1, 1))
        )

    residual = to_row(gradient_sum) - roughness(cond_row, static_in[0, 0:1, :], static_in[1, 0:1, :])
    residual = jnp.where(own, residual, 0.0)

    quarter = core + 2 * (cell % 2)
    weights = jnp.concatenate([setup_in[block, 4:5, :] for block in range(DP)], axis=0)

    def finish_step(step, held):
        await_bytes(scalar_in.at[step, pl.ds(63, 7)], recv_sems.at[2 + 5 * step + 4])
        sums = held["scalars"] + jnp.sum(scalar_in[step, 63:70], axis=0)
        norm, energy = sums[:, 0:1], sums[:, 1:2]
        predicted, rough, whole = held["image"], held["rough"], held["plane"]
        ratio = None
        if step > 0:
            ratio = norm / held["norm"]
            energy = energy + ratio * (2.0 * sums[:, 2:3] + ratio * held["energy"])
            predicted = predicted + ratio * held["predicted"]
            rough = rough + ratio * held["direction_rough"]
            whole = whole + ratio * held["whole"]
        square = jnp.sum(weights * predicted * predicted, axis=0, keepdims=True)
        length = norm / (energy + lane_sum(square))
        update, change = length * whole, length * predicted
        if step > 0:
            update, change = held["update"] + update, held["change"] + change
        held.update(
            norm=norm,
            energy=energy,
            predicted=predicted,
            direction_rough=rough,
            whole=whole,
            update=update,
            change=change,
        )
        return ratio, length

    def along(name, value, ratio, held):
        held[name] = value if ratio is None else value + ratio * held[name]
        return held[name]

    held = {}
    vector = residual
    for it in range(ITERS):
        sem = 2 + 5 * it
        halo_out[it] = vector
        for slot, (to_dp, to_cell) in enumerate(
            (
                (dp, above),
                (dp, below),
                ((dp + 1) % DP, cell),
                ((dp + DP - 1) % DP, cell),
            )
        ):
            push(
                halo_out.at[it],
                halo_in.at[it, slot],
                send_sems.at[sem],
                recv_sems.at[sem],
                to_dp,
                to_cell,
            )
        column = jnp.broadcast_to(to_column(vector), (OWN, LANES))
        for part in range(4):
            first_out[it, part] = jnp.concatenate(
                [
                    jnp.sum(sens[4 * part + row] * column, axis=0, keepdims=True)
                    for row in range(4)
                ],
                axis=0,
            )
        for slot, (to_core, to_x, to_y) in enumerate(PLANE):
            to_dp = 2 * chip + (core + to_core) % 2
            to_cell = (cell // 8 + to_x) % 4 * 8 + (cell + to_y) % 8
            push(
                first_out.at[it, to_dp % 2 + 2 * (to_cell % 2)],
                first_in.at[it, slot],
                send_sems.at[sem + 1],
                recv_sems.at[sem + 1],
                to_dp,
                to_cell,
            )

        if it > 0:
            ratio, length = finish_step(it - 1, held)
            residual = residual - length * along("hessian", vector, ratio, held)

        await_bytes(halo_in.at[it], recv_sems.at[sem])
        before, after = halo_in[it, 2], halo_in[it, 3]
        wide = jnp.where(own, vector, pltpu.roll(jnp.where(lane >= 64, before, after), 64, 1))
        rough = roughness(wide, halo_in[it, 0], halo_in[it, 1]) + DAMPING * vector
        if it > 0:
            rough = held["rough"] - length * along("hessian_rough", rough, ratio, held)
        held["rough"] = rough
        scalars = jnp.where(lane == 0, lane_sum(residual * residual), 0.0)
        scalars = jnp.where(lane == 1, lane_sum(residual * rough), scalars)
        if it > 0:
            scalars = jnp.where(lane == 2, lane_sum(residual * held["direction_rough"]), scalars)
        scalar_out[it, 0] = scalars
        for slot, (to_core, to_x, to_y) in enumerate(PLANE):
            push(
                scalar_out.at[it, 0],
                scalar_in.at[it, slot],
                send_sems.at[sem + 3],
                recv_sems.at[sem + 3],
                2 * chip + (core + to_core) % 2,
                (cell // 8 + to_x) % 4 * 8 + (cell + to_y) % 8,
            )

        await_bytes(first_in.at[it], recv_sems.at[sem + 1])
        partial = first_out[it, quarter] + jnp.sum(first_in[it], axis=0)
        second_in[it, 4 * chip + quarter] = jnp.concatenate([partial, residual], axis=0)
        for to_z, to_core, to_pair in COLUMN:
            push(
                second_in.at[it, 4 * chip + quarter],
                second_in.at[it, 4 * chip + quarter],
                send_sems.at[sem + 2],
                recv_sems.at[sem + 2],
                (chip + to_z) % 8 * 2 + (core + to_core) % 2,
                cell + to_pair * (1 - 2 * (cell % 2)),
            )

        await_bytes(scalar_in.at[it, pl.ds(0, 63)], recv_sems.at[sem + 3])
        scalars = scalars + jnp.sum(scalar_in[it, 0:63], axis=0)
        scalar_out[it, 1] = scalars
        for slot, to_z in enumerate((4, 3, 5, 2, 6, 1, 7)):
            push(
                scalar_out.at[it, 1],
                scalar_in.at[it, 63 + slot],
                send_sems.at[sem + 4],
                recv_sems.at[sem + 4],
                (chip + to_z) % 8 * 2 + core,
                cell,
            )

        held["scalars"] = scalars

        await_bytes(second_in.at[it, pl.ds(0, 31)], recv_sems.at[sem + 2])
        quarters = [second_in[it, part] for part in range(4)]
        for plane in range(1, 8):
            for part in range(4):
                quarters[part] += second_in[it, 4 * plane + part]
        image = jnp.concatenate([rows[0:4] for rows in quarters], axis=0)
        if it > 0:
            image = held["image"] - length * along("hessian_image", image, ratio, held)
        held["image"] = image
        if it < ITERS - 1:
            weighted = weights * image
            spread = sens[0] * weighted[0:1]
            for block in range(1, DP):
                spread += sens[block] * weighted[block : block + 1]
            vector = jnp.where(own, to_row(spread) + rough, 0.0)
        held["plane"] = jnp.concatenate(
            [
                second_in[it, source // 2 * 4 + source % 2 + 2 * (cell % 2)][4:5]
                for source in range(DP)
            ],
            axis=0,
        )

    finish_step(ITERS - 1, held)
    update, change = held["update"], held["change"]
    update_out[...] = update
    mine = lax.broadcasted_iota(jnp.int32, (DP, LANES), 0) == dp
    change_out[...] = jnp.sum(jnp.where(mine, change, 0.0), axis=0, keepdims=True)

    await_bytes(setup_in.at[pl.ds(0, DP - 1)], send_sems.at[0])
    await_bytes(static_in, send_sems.at[1])
    await_bytes(field_in.at[pl.ds(0, DP - 1)], field_send)
    for it in range(ITERS):
        sem = 2 + 5 * it
        await_bytes(halo_in.at[it], send_sems.at[sem])
        await_bytes(first_in.at[it], send_sems.at[sem + 1])
        await_bytes(second_in.at[it, pl.ds(0, 31)], send_sems.at[sem + 2])
        await_bytes(scalar_in.at[it, pl.ds(0, 63)], send_sems.at[sem + 3])
        await_bytes(scalar_in.at[it, pl.ds(63, 7)], send_sems.at[sem + 4])


def per_device(configs, pole_fields, misfit, data_weight, conductivity, face_weights):
    vmem = pl.BlockSpec(memory_space=pltpu.VMEM)
    update, change = pl.pallas_call(
        kernel,
        name="inversion",
        out_shape=(
            jax.ShapeDtypeStruct((DP, LANES), F32),
            jax.ShapeDtypeStruct((1, LANES), F32),
        ),
        in_specs=[pl.BlockSpec(memory_space=pltpu.HBM)] * 6,
        out_specs=(vmem, vmem),
        scratch_shapes=[
            pltpu.VMEM((3, POLE_ROWS, 8 * LANES), BF16),
            pltpu.VMEM((4, LANES), jnp.int32),
            pltpu.VMEM((1, LANES), F32),
            pltpu.VMEM((1, LANES), F32),
            pltpu.VMEM((8, LANES), F32),
            pltpu.VMEM((3, 8 * LANES), F32),
            pltpu.VMEM((DP, 3 * OWN, POLE_ROWS), BF16),
            pltpu.VMEM((DP, 3 * OWN, POLE_ROWS), BF16),
            pltpu.VMEM((CHUNK, 2 * DATA), BF16),
            pltpu.VMEM((CHUNK, 2 * DATA), BF16),
            pltpu.VMEM((3 * OWN, 2 * DATA), F32),
            pltpu.VMEM((DP, OWN, LANES), F32),
            pltpu.VMEM((8, LANES), F32),
            pltpu.VMEM((DP, 8, LANES), F32),
            pltpu.VMEM((2, LANES), F32),
            pltpu.VMEM((2, 2, LANES), F32),
            pltpu.VMEM((ITERS, 1, LANES), F32),
            pltpu.VMEM((ITERS, 4, 1, LANES), F32),
            pltpu.VMEM((ITERS, 4, 4, LANES), F32),
            pltpu.VMEM((ITERS, 63, 4, LANES), F32),
            pltpu.VMEM((ITERS, 32, 5, LANES), F32),
            pltpu.VMEM((ITERS, 2, 1, LANES), F32),
            pltpu.VMEM((ITERS, 70, 1, LANES), F32),
            pltpu.SemaphoreType.DMA,
            pltpu.SemaphoreType.DMA((DP,)),
            pltpu.SemaphoreType.DMA((2 + 5 * ITERS,)),
            pltpu.SemaphoreType.DMA((2 + 5 * ITERS,)),
            pltpu.SemaphoreType.DMA((6,)),
        ],
        compiler_params=pltpu.CompilerParams(
            collective_id=0, has_side_effects=True, vmem_limit_bytes=40 * 1024 * 1024
        ),
    )(
        pole_fields,
        configs.T,
        misfit.reshape(1, LANES),
        data_weight.reshape(1, LANES),
        conductivity.reshape(8, LANES),
        face_weights,
    )
    return update[:, 32:96].reshape(-1), change.reshape(-1)


def solution(mesh):
    placed = (P("dp", None), P(None, "dp", "cell"), P("dp"), P("dp"), P("cell"), P(None, "cell"))
    return jax.shard_map(
        per_device, mesh=mesh, in_specs=placed, out_specs=(P("cell"), P("dp")), check_vma=False
    )
```

```python
import functools
import math

import jax
import jax.numpy as jnp
from jax import lax
from jax.experimental import pallas as pl
from jax.experimental.pallas import tpu as pltpu
from jax.sharding import PartitionSpec as P

GY = 32
GZ = 32
ITERS = 3
DAMPING = 0.2

DP = 16
CELL = 32
OWN = 64
POLE_ROWS = 128
CHUNK = 256
DATA = 2048
LANES = 128
F32 = jnp.float32
BF16 = jnp.bfloat16
MESH = pl.DeviceIdType.MESH

FAR = (4, 3, 5, 2, 6, 1, 7, 0)
PLANE = [(c, x, y) for x in (2, 1, 3, 0) for y in FAR for c in (0, 1) if (c, x, y) != (0, 0, 0)]
COLUMN = [(z, c, y) for z in FAR for y in (1, 0) for c in (0, 1) if (z, c, y) != (0, 0, 0)]


def lane_sum(row):
    return jnp.sum(row, axis=1, keepdims=True)


def kernel(
    fields_hbm,
    configs_hbm,
    misfit_hbm,
    weight_hbm,
    conductivity_hbm,
    faces_hbm,
    update_out,
    change_out,
    fields,
    configs_t,
    misfit,
    weight,
    conductivity,
    faces,
    field_out,
    field_in,
    signs_a,
    signs_b,
    totals,
    sens,
    setup_out,
    setup_in,
    static_out,
    static_in,
    halo_out,
    halo_in,
    first_out,
    first_in,
    second_in,
    scalar_out,
    scalar_in,
    field_send,
    field_recv,
    send_sems,
    recv_sems,
    load_sems,
):
    loads = []
    for index, (source, target) in enumerate(
        (
            (fields_hbm, fields),
            (configs_hbm, configs_t),
            (weight_hbm, weight),
            (misfit_hbm, misfit),
            (conductivity_hbm, conductivity),
            (faces_hbm, faces),
        )
    ):
        loads.append(pltpu.make_async_copy(source, target, load_sems.at[index]))
        loads[-1].start()

    dp = lax.axis_index("dp")
    cell = lax.axis_index("cell")
    chip = dp // 2
    core = dp % 2
    above = (cell + 1) % CELL
    below = (cell + CELL - 1) % CELL

    barrier = pltpu.get_barrier_semaphore()
    for to_core, to_x, to_y in PLANE:
        pl.semaphore_signal(
            barrier,
            inc=1,
            device_id={
                "dp": 2 * chip + (core + to_core) % 2,
                "cell": (cell // 8 + to_x) % 4 * 8 + (cell + to_y) % 8,
            },
            device_id_type=MESH,
        )
    for to_z, to_core, to_pair in COLUMN:
        if to_z != 0:
            pl.semaphore_signal(
                barrier,
                inc=1,
                device_id={
                    "dp": (chip + to_z) % 8 * 2 + (core + to_core) % 2,
                    "cell": cell + to_pair * (1 - 2 * (cell % 2)),
                },
                device_id_type=MESH,
            )

    lane = lax.broadcasted_iota(jnp.int32, (1, LANES), 1)
    own = (lane >= 32) & (lane < 96)

    for load in loads:
        load.wait()

    for target in range(8):
        for part in range(3):
            turned = fields[part, :, target * LANES : (target + 1) * LANES].T
            field_out[2 * target, part * OWN : (part + 1) * OWN, :] = turned[:OWN]
            field_out[2 * target + 1, part * OWN : (part + 1) * OWN, :] = turned[OWN:]
    field_in[dp] = field_out[dp]

    setup_out[0:4, :] = configs_t[...].astype(F32)
    setup_out[4:5, :] = weight[...]
    setup_out[5:6, :] = misfit[...]
    setup_out[6:8, :] = jnp.zeros((2, LANES), F32)
    setup_in[dp] = setup_out[...]

    even = dp % 2 == 0
    tile_a = jnp.maximum((dp + 1) // 2 - 1, 0)
    tile_b = jnp.minimum((dp + 1) // 2, 7)

    def widened(first, second):
        if_even = jnp.where(lane < 32, pltpu.roll(first, 32, 1), pltpu.roll(second, 32, 1))
        if_odd = jnp.where(lane < 96, pltpu.roll(first, 96, 1), pltpu.roll(second, 96, 1))
        return jnp.where(jnp.broadcast_to(even, (1, LANES)), if_even, if_odd)

    def face_row(axis):
        return widened(
            faces[axis : axis + 1, pl.ds(pl.multiple_of(tile_a * LANES, LANES), LANES)],
            faces[axis : axis + 1, pl.ds(pl.multiple_of(tile_b * LANES, LANES), LANES)],
        )

    cond_row = widened(conductivity[pl.ds(tile_a, 1), :], conductivity[pl.ds(tile_b, 1), :])
    face_x, face_y, face_z = face_row(0), face_row(1), face_row(2)
    static_out[0:1, :] = cond_row
    static_out[1:2, :] = face_x

    pl.semaphore_wait(barrier, 63 + 28)

    def push(source, target, send, recv, to_dp, to_cell):
        pltpu.make_async_remote_copy(
            src_ref=source,
            dst_ref=target,
            send_sem=send,
            recv_sem=recv,
            device_id={"dp": to_dp, "cell": to_cell},
            device_id_type=MESH,
        ).start()

    def await_bytes(ref, sem):
        pltpu.make_async_copy(ref, ref, sem).wait()

    for step in range(1, DP):
        push(setup_out, setup_in.at[dp], send_sems.at[0], recv_sems.at[0], (dp + step) % DP, cell)
    push(static_out, static_in.at[0], send_sems.at[1], recv_sems.at[1], dp, above)
    push(static_out, static_in.at[1], send_sems.at[1], recv_sems.at[1], dp, below)
    for far in (1, 7, 2, 6, 3, 5, 4, 0):
        for other in (0, 1):
            if (far, other) == (0, 0):
                continue
            to = (chip + far) % 8 * 2 + (core + other) % 2
            push(field_out.at[to], field_in.at[dp], field_send, field_recv.at[dp], to, cell)

    await_bytes(setup_in.at[pl.ds(0, DP - 1)], recv_sems.at[0])

    def chunk_of(step):
        half = (step + 1) // 2
        return (chip + (8 - half) % 8 + (step % 2) * (2 * half - 8)) % 8

    def build(signs, step):
        ids = lax.broadcasted_iota(jnp.int32, (CHUNK, 1), 0) + chunk_of(step) * CHUNK
        ids = jnp.broadcast_to(ids.astype(F32), (CHUNK, LANES))
        for block in range(DP):
            for pair in range(2):
                plus = setup_in[block, 2 * pair : 2 * pair + 1, :]
                minus = setup_in[block, 2 * pair + 1 : 2 * pair + 2, :]
                value = jnp.where(ids == plus, 1.0, jnp.where(ids == minus, -1.0, 0.0))
                at = pair * DATA + block * LANES
                signs[:, at : at + LANES] = value.astype(BF16)

    def product(signs, step):
        chunk = chunk_of(step)
        left = jnp.concatenate([field_in[2 * chunk], field_in[2 * chunk + 1]], axis=1)
        return jnp.dot(left, signs[...], preferred_element_type=F32)

    def await_fields(step):
        for part in range(2):
            source = 2 * chunk_of(step) + part
            await_bytes(field_in.at[source], field_recv.at[source])

    build(signs_a, 0)
    sibling = 2 * chip + 1 - core
    await_bytes(field_in.at[sibling], field_recv.at[sibling])
    totals[...] = product(signs_a, 0)
    build(signs_b, 1)

    def two_chunks(turn, carry):
        for signs, later, step in (
            (signs_b, signs_a, 2 * turn + 1),
            (signs_a, signs_b, 2 * turn + 2),
        ):
            await_fields(step)
            totals[...] += product(signs, step)
            build(later, step + 1)
        return carry

    lax.fori_loop(0, 3, two_chunks, 0)
    await_fields(7)
    totals[...] += product(signs_b, 7)

    scale = -1.0 / math.sqrt(DATA)
    gradient_sum = jnp.zeros((OWN, LANES), F32)
    for block in range(DP):
        at, bt = block * LANES, DATA + block * LANES
        value = totals[0:OWN, at : at + LANES] * totals[0:OWN, bt : bt + LANES]
        for part in (1, 2):
            rows = slice(part * OWN, (part + 1) * OWN)
            value += totals[rows, at : at + LANES] * totals[rows, bt : bt + LANES]
        value = value * scale
        sens[block] = value
        gradient_sum += value * (setup_in[block, 4:5, :] * setup_in[block, 5:6, :])

    spot = lax.broadcasted_iota(jnp.int32, (OWN, LANES), 0) + 32 == lax.broadcasted_iota(
        jnp.int32, (OWN, LANES), 1
    )

    def to_row(spread):
        column = jnp.sum(spread, axis=1, keepdims=True)
        return jnp.sum(jnp.where(spot, column, 0.0), axis=0, keepdims=True)

    def to_column(row):
        return jnp.sum(jnp.where(spot, row, 0.0), axis=1, keepdims=True)

    await_bytes(static_in, recv_sems.at[1])

    def masked(row, keep):
        return jnp.where(own & keep, row, 0.0)

    grid_y = 2 * dp + (lane - 32) // 32
    grid_z = lane % 32
    up_x = masked(face_x, jnp.broadcast_to(cell < CELL - 1, (1, LANES)))
    low_x = masked(static_in[0, 1:2, :], jnp.broadcast_to(cell > 0, (1, LANES)))
    up_y = masked(face_y, grid_y < GY - 1)
    low_y = masked(pltpu.roll(face_y, 32, 1), grid_y > 0)
    up_z = masked(face_z, grid_z < GZ - 1)
    low_z = masked(pltpu.roll(face_z, 1, 1), grid_z > 0)

    def roughness(row, lower, upper):
        return (
            up_x * (row - upper)
            + low_x * (row - lower)
            + up_y * (row - pltpu.roll(row, 96, 1))
            + low_y * (row - pltpu.roll(row, 32, 1))
            + up_z * (row - pltpu.roll(row, 127, 1))
            + low_z * (row - pltpu.roll(row, 1, 1))
        )

    residual = to_row(gradient_sum) - roughness(cond_row, static_in[0, 0:1, :], static_in[1, 0:1, :])
    residual = jnp.where(own, residual, 0.0)

    quarter = core + 2 * (cell % 2)
    weights = jnp.concatenate([setup_in[block, 4:5, :] for block in range(DP)], axis=0)

    def finish_step(step, held):
        await_bytes(scalar_in.at[step, pl.ds(63, 7)], recv_sems.at[2 + 5 * step + 4])
        sums = held["scalars"] + jnp.sum(scalar_in[step, 63:70], axis=0)
        norm, energy = sums[:, 0:1], sums[:, 1:2]
        predicted, rough, whole = held["image"], held["rough"], held["plane"]
        ratio = None
        if step > 0:
            ratio = norm / held["norm"]
            energy = energy + ratio * (2.0 * sums[:, 2:3] + ratio * held["energy"])
            predicted = predicted + ratio * held["predicted"]
            rough = rough + ratio * held["direction_rough"]
            whole = whole + ratio * held["whole"]
        square = jnp.sum(weights * predicted * predicted, axis=0, keepdims=True)
        length = norm / (energy + lane_sum(square))
        update, change = length * whole, length * predicted
        if step > 0:
            update, change = held["update"] + update, held["change"] + change
        held.update(
            norm=norm,
            energy=energy,
            predicted=predicted,
            direction_rough=rough,
            whole=whole,
            update=update,
            change=change,
        )
        return ratio, length

    def along(name, value, ratio, held):
        held[name] = value if ratio is None else value + ratio * held[name]
        return held[name]

    held = {}
    vector = residual
    for it in range(ITERS):
        sem = 2 + 5 * it
        halo_out[it] = vector
        for slot, (to_dp, to_cell) in enumerate(
            (
                (dp, above),
                (dp, below),
                ((dp + 1) % DP, cell),
                ((dp + DP - 1) % DP, cell),
            )
        ):
            push(
                halo_out.at[it],
                halo_in.at[it, slot],
                send_sems.at[sem],
                recv_sems.at[sem],
                to_dp,
                to_cell,
            )
        column = jnp.broadcast_to(to_column(vector), (OWN, LANES))
        for part in range(4):
            first_out[it, part] = jnp.concatenate(
                [
                    jnp.sum(sens[4 * part + row] * column, axis=0, keepdims=True)
                    for row in range(4)
                ],
                axis=0,
            )
        for slot, (to_core, to_x, to_y) in enumerate(PLANE):
            to_dp = 2 * chip + (core + to_core) % 2
            to_cell = (cell // 8 + to_x) % 4 * 8 + (cell + to_y) % 8
            push(
                first_out.at[it, to_dp % 2 + 2 * (to_cell % 2)],
                first_in.at[it, slot],
                send_sems.at[sem + 1],
                recv_sems.at[sem + 1],
                to_dp,
                to_cell,
            )

        if it > 0:
            ratio, length = finish_step(it - 1, held)
            residual = residual - length * along("hessian", vector, ratio, held)

        await_bytes(halo_in.at[it], recv_sems.at[sem])
        before, after = halo_in[it, 2], halo_in[it, 3]
        wide = jnp.where(own, vector, pltpu.roll(jnp.where(lane >= 64, before, after), 64, 1))
        rough = roughness(wide, halo_in[it, 0], halo_in[it, 1]) + DAMPING * vector
        if it > 0:
            rough = held["rough"] - length * along("hessian_rough", rough, ratio, held)
        held["rough"] = rough
        scalars = jnp.where(lane == 0, lane_sum(residual * residual), 0.0)
        scalars = jnp.where(lane == 1, lane_sum(residual * rough), scalars)
        if it > 0:
            scalars = jnp.where(lane == 2, lane_sum(residual * held["direction_rough"]), scalars)
        scalar_out[it, 0] = scalars
        for slot, (to_core, to_x, to_y) in enumerate(PLANE):
            push(
                scalar_out.at[it, 0],
                scalar_in.at[it, slot],
                send_sems.at[sem + 3],
                recv_sems.at[sem + 3],
                2 * chip + (core + to_core) % 2,
                (cell // 8 + to_x) % 4 * 8 + (cell + to_y) % 8,
            )

        await_bytes(first_in.at[it], recv_sems.at[sem + 1])
        partial = first_out[it, quarter] + jnp.sum(first_in[it], axis=0)
        second_in[it, 4 * chip + quarter] = jnp.concatenate([partial, residual], axis=0)
        for to_z, to_core, to_pair in COLUMN:
            push(
                second_in.at[it, 4 * chip + quarter],
                second_in.at[it, 4 * chip + quarter],
                send_sems.at[sem + 2],
                recv_sems.at[sem + 2],
                (chip + to_z) % 8 * 2 + (core + to_core) % 2,
                cell + to_pair * (1 - 2 * (cell % 2)),
            )

        await_bytes(scalar_in.at[it, pl.ds(0, 63)], recv_sems.at[sem + 3])
        scalars = scalars + jnp.sum(scalar_in[it, 0:63], axis=0)
        scalar_out[it, 1] = scalars
        for slot, to_z in enumerate((4, 3, 5, 2, 6, 1, 7)):
            push(
                scalar_out.at[it, 1],
                scalar_in.at[it, 63 + slot],
                send_sems.at[sem + 4],
                recv_sems.at[sem + 4],
                (chip + to_z) % 8 * 2 + core,
                cell,
            )

        held["scalars"] = scalars

        await_bytes(second_in.at[it, pl.ds(0, 31)], recv_sems.at[sem + 2])
        quarters = [second_in[it, part] for part in range(4)]
        for plane in range(1, 8):
            for part in range(4):
                quarters[part] += second_in[it, 4 * plane + part]
        image = jnp.concatenate([rows[0:4] for rows in quarters], axis=0)
        if it > 0:
            image = held["image"] - length * along("hessian_image", image, ratio, held)
        held["image"] = image
        if it < ITERS - 1:
            weighted = weights * image
            spread = sens[0] * weighted[0:1]
            for block in range(1, DP):
                spread += sens[block] * weighted[block : block + 1]
            vector = jnp.where(own, to_row(spread) + rough, 0.0)
        mine = [
            second_in[it, source // 2 * 4 + source % 2 + 2 * (cell % 2)][4:5]
            for source in range(DP)
        ]
        left = pltpu.roll(jnp.concatenate(mine[0::2], axis=0), 96, 1)
        right = pltpu.roll(jnp.concatenate(mine[1::2], axis=0), 32, 1)
        held["plane"] = jnp.where(lane < 64, left, right)

    finish_step(ITERS - 1, held)
    update, change = held["update"], held["change"]
    update_out[...] = update
    mine = lax.broadcasted_iota(jnp.int32, (DP, LANES), 0) == dp
    change_out[...] = jnp.sum(jnp.where(mine, change, 0.0), axis=0, keepdims=True)

    await_bytes(setup_in.at[pl.ds(0, DP - 1)], send_sems.at[0])
    await_bytes(static_in, send_sems.at[1])
    await_bytes(field_in.at[pl.ds(0, DP - 1)], field_send)
    for it in range(ITERS):
        sem = 2 + 5 * it
        await_bytes(halo_in.at[it], send_sems.at[sem])
        await_bytes(first_in.at[it], send_sems.at[sem + 1])
        await_bytes(second_in.at[it, pl.ds(0, 31)], send_sems.at[sem + 2])
        await_bytes(scalar_in.at[it, pl.ds(0, 63)], send_sems.at[sem + 3])
        await_bytes(scalar_in.at[it, pl.ds(63, 7)], send_sems.at[sem + 4])


def per_device(configs, pole_fields, misfit, data_weight, conductivity, face_weights):
    vmem = pl.BlockSpec(memory_space=pltpu.VMEM)
    update, change = pl.pallas_call(
        kernel,
        name="inversion",
        out_shape=(
            jax.ShapeDtypeStruct((8, LANES), F32),
            jax.ShapeDtypeStruct((1, LANES), F32),
        ),
        in_specs=[pl.BlockSpec(memory_space=pltpu.HBM)] * 6,
        out_specs=(vmem, vmem),
        scratch_shapes=[
            pltpu.VMEM((3, POLE_ROWS, 8 * LANES), BF16),
            pltpu.VMEM((4, LANES), jnp.int32),
            pltpu.VMEM((1, LANES), F32),
            pltpu.VMEM((1, LANES), F32),
            pltpu.VMEM((8, LANES), F32),
            pltpu.VMEM((3, 8 * LANES), F32),
            pltpu.VMEM((DP, 3 * OWN, POLE_ROWS), BF16),
            pltpu.VMEM((DP, 3 * OWN, POLE_ROWS), BF16),
            pltpu.VMEM((CHUNK, 2 * DATA), BF16),
            pltpu.VMEM((CHUNK, 2 * DATA), BF16),
            pltpu.VMEM((3 * OWN, 2 * DATA), F32),
            pltpu.VMEM((DP, OWN, LANES), F32),
            pltpu.VMEM((8, LANES), F32),
            pltpu.VMEM((DP, 8, LANES), F32),
            pltpu.VMEM((2, LANES), F32),
            pltpu.VMEM((2, 2, LANES), F32),
            pltpu.VMEM((ITERS, 1, LANES), F32),
            pltpu.VMEM((ITERS, 4, 1, LANES), F32),
            pltpu.VMEM((ITERS, 4, 4, LANES), F32),
            pltpu.VMEM((ITERS, 63, 4, LANES), F32),
            pltpu.VMEM((ITERS, 32, 5, LANES), F32),
            pltpu.VMEM((ITERS, 2, 1, LANES), F32),
            pltpu.VMEM((ITERS, 70, 1, LANES), F32),
            pltpu.SemaphoreType.DMA,
            pltpu.SemaphoreType.DMA((DP,)),
            pltpu.SemaphoreType.DMA((2 + 5 * ITERS,)),
            pltpu.SemaphoreType.DMA((2 + 5 * ITERS,)),
            pltpu.SemaphoreType.DMA((6,)),
        ],
        compiler_params=pltpu.CompilerParams(
            collective_id=0, has_side_effects=True, vmem_limit_bytes=60 * 1024 * 1024
        ),
    )(
        pole_fields,
        configs.T,
        misfit.reshape(1, LANES),
        data_weight.reshape(1, LANES),
        conductivity.reshape(8, LANES),
        face_weights,
    )
    return update.reshape(-1), change.reshape(-1)


def solution(mesh):
    placed = (P("dp", None), P(None, "dp", "cell"), P("dp"), P("dp"), P("cell"), P(None, "cell"))
    return jax.shard_map(
        per_device, mesh=mesh, in_specs=placed, out_specs=(P("cell"), P("dp")), check_vma=False
    )
```

```python
import functools
import math

import jax
import jax.numpy as jnp
from jax import lax
from jax.experimental import pallas as pl
from jax.experimental.pallas import tpu as pltpu
from jax.sharding import PartitionSpec as P

GY = 32
GZ = 32
ITERS = 3
DAMPING = 0.2

DP = 16
CELL = 32
OWN = 64
POLE_ROWS = 128
CHUNK = 256
DATA = 2048
LANES = 128
F32 = jnp.float32
BF16 = jnp.bfloat16
MESH = pl.DeviceIdType.MESH

FAR = (4, 3, 5, 2, 6, 1, 7, 0)
PLANE = [(c, x, y) for x in (2, 1, 3, 0) for y in FAR for c in (0, 1) if (c, x, y) != (0, 0, 0)]
COLUMN = [(z, c, y) for z in FAR for y in (1, 0) for c in (0, 1) if (z, c, y) != (0, 0, 0)]


def lane_sum(row):
    return jnp.sum(row, axis=1, keepdims=True)


def kernel(
    fields_hbm,
    configs_hbm,
    misfit_hbm,
    weight_hbm,
    conductivity_hbm,
    faces_hbm,
    update_out,
    change_out,
    fields,
    configs_t,
    misfit,
    weight,
    conductivity,
    faces,
    field_out,
    field_in,
    signs_a,
    signs_b,
    totals,
    sens,
    setup_out,
    setup_in,
    static_out,
    static_in,
    halo_out,
    halo_in,
    first_out,
    first_in,
    second_in,
    scalar_out,
    scalar_in,
    field_send,
    field_recv,
    send_sems,
    recv_sems,
    load_sems,
):
    loads = []
    for index, (source, target) in enumerate(
        (
            (fields_hbm, fields),
            (configs_hbm, configs_t),
            (weight_hbm, weight),
            (misfit_hbm, misfit),
            (conductivity_hbm, conductivity),
            (faces_hbm, faces),
        )
    ):
        loads.append(pltpu.make_async_copy(source, target, load_sems.at[index]))
        loads[-1].start()

    dp = lax.axis_index("dp")
    cell = lax.axis_index("cell")
    chip = dp // 2
    core = dp % 2
    above = (cell + 1) % CELL
    below = (cell + CELL - 1) % CELL

    barrier = pltpu.get_barrier_semaphore()
    for to_core, to_x, to_y in PLANE:
        pl.semaphore_signal(
            barrier,
            inc=1,
            device_id={
                "dp": 2 * chip + (core + to_core) % 2,
                "cell": (cell // 8 + to_x) % 4 * 8 + (cell + to_y) % 8,
            },
            device_id_type=MESH,
        )
    for to_z, to_core, to_pair in COLUMN:
        if to_z != 0:
            pl.semaphore_signal(
                barrier,
                inc=1,
                device_id={
                    "dp": (chip + to_z) % 8 * 2 + (core + to_core) % 2,
                    "cell": cell + to_pair * (1 - 2 * (cell % 2)),
                },
                device_id_type=MESH,
            )

    lane = lax.broadcasted_iota(jnp.int32, (1, LANES), 1)
    own = (lane >= 32) & (lane < 96)

    for load in loads:
        load.wait()

    for target in range(8):
        for part in range(3):
            turned = fields[part, :, target * LANES : (target + 1) * LANES].T
            field_out[2 * target, part * OWN : (part + 1) * OWN, :] = turned[:OWN]
            field_out[2 * target + 1, part * OWN : (part + 1) * OWN, :] = turned[OWN:]
    field_in[dp] = field_out[dp]

    setup_out[0:4, :] = configs_t[...].astype(F32)
    setup_out[4:5, :] = weight[...]
    setup_out[5:6, :] = misfit[...]
    setup_out[6:8, :] = jnp.zeros((2, LANES), F32)
    setup_in[dp] = setup_out[...]

    even = dp % 2 == 0
    tile_a = jnp.maximum((dp + 1) // 2 - 1, 0)
    tile_b = jnp.minimum((dp + 1) // 2, 7)

    def widened(first, second):
        if_even = jnp.where(lane < 32, pltpu.roll(first, 32, 1), pltpu.roll(second, 32, 1))
        if_odd = jnp.where(lane < 96, pltpu.roll(first, 96, 1), pltpu.roll(second, 96, 1))
        return jnp.where(jnp.broadcast_to(even, (1, LANES)), if_even, if_odd)

    def face_row(axis):
        return widened(
            faces[axis : axis + 1, pl.ds(pl.multiple_of(tile_a * LANES, LANES), LANES)],
            faces[axis : axis + 1, pl.ds(pl.multiple_of(tile_b * LANES, LANES), LANES)],
        )

    cond_row = widened(conductivity[pl.ds(tile_a, 1), :], conductivity[pl.ds(tile_b, 1), :])
    face_x, face_y, face_z = face_row(0), face_row(1), face_row(2)
    static_out[0:1, :] = cond_row
    static_out[1:2, :] = face_x

    pl.semaphore_wait(barrier, 63 + 28)

    def push(source, target, send, recv, to_dp, to_cell):
        pltpu.make_async_remote_copy(
            src_ref=source,
            dst_ref=target,
            send_sem=send,
            recv_sem=recv,
            device_id={"dp": to_dp, "cell": to_cell},
            device_id_type=MESH,
        ).start()

    def await_bytes(ref, sem):
        pltpu.make_async_copy(ref, ref, sem).wait()

    for step in range(1, DP):
        push(setup_out, setup_in.at[dp], send_sems.at[0], recv_sems.at[0], (dp + step) % DP, cell)
    push(static_out, static_in.at[0], send_sems.at[1], recv_sems.at[1], dp, above)
    push(static_out, static_in.at[1], send_sems.at[1], recv_sems.at[1], dp, below)
    for far in (1, 7, 2, 6, 3, 5, 4, 0):
        for other in (0, 1):
            if (far, other) == (0, 0):
                continue
            to = (chip + far) % 8 * 2 + (core + other) % 2
            push(field_out.at[to], field_in.at[dp], field_send, field_recv.at[dp], to, cell)

    await_bytes(setup_in.at[pl.ds(0, DP - 1)], recv_sems.at[0])

    def chunk_of(step):
        half = (step + 1) // 2
        return (chip + (8 - half) % 8 + (step % 2) * (2 * half - 8)) % 8

    def build(signs, step):
        ids = lax.broadcasted_iota(jnp.int32, (CHUNK, 1), 0) + chunk_of(step) * CHUNK
        ids = jnp.broadcast_to(ids.astype(F32), (CHUNK, LANES))
        for block in range(DP):
            for pair in range(2):
                plus = setup_in[block, 2 * pair : 2 * pair + 1, :]
                minus = setup_in[block, 2 * pair + 1 : 2 * pair + 2, :]
                value = jnp.where(ids == plus, 1.0, jnp.where(ids == minus, -1.0, 0.0))
                at = pair * DATA + block * LANES
                signs[:, at : at + LANES] = value.astype(BF16)

    def product(signs, step):
        chunk = chunk_of(step)
        left = jnp.concatenate([field_in[2 * chunk], field_in[2 * chunk + 1]], axis=1)
        return jnp.dot(left, signs[...], preferred_element_type=F32)

    def await_fields(step):
        for part in range(2):
            source = 2 * chunk_of(step) + part
            await_bytes(field_in.at[source], field_recv.at[source])

    build(signs_a, 0)
    sibling = 2 * chip + 1 - core
    await_bytes(field_in.at[sibling], field_recv.at[sibling])
    totals[...] = product(signs_a, 0)
    build(signs_b, 1)

    def two_chunks(turn, carry):
        for signs, later, step in (
            (signs_b, signs_a, 2 * turn + 1),
            (signs_a, signs_b, 2 * turn + 2),
        ):
            await_fields(step)
            totals[...] += product(signs, step)
            build(later, step + 1)
        return carry

    lax.fori_loop(0, 3, two_chunks, 0)
    await_fields(7)
    totals[...] += product(signs_b, 7)

    scale = -1.0 / math.sqrt(DATA)
    gradient_sum = jnp.zeros((OWN, LANES), F32)
    for block in range(DP):
        at, bt = block * LANES, DATA + block * LANES
        value = totals[0:OWN, at : at + LANES] * totals[0:OWN, bt : bt + LANES]
        for part in (1, 2):
            rows = slice(part * OWN, (part + 1) * OWN)
            value += totals[rows, at : at + LANES] * totals[rows, bt : bt + LANES]
        value = value * scale
        sens[block] = value
        gradient_sum += value * (setup_in[block, 4:5, :] * setup_in[block, 5:6, :])

    spot = lax.broadcasted_iota(jnp.int32, (OWN, LANES), 0) + 32 == lax.broadcasted_iota(
        jnp.int32, (OWN, LANES), 1
    )

    def to_row(spread):
        column = jnp.sum(spread, axis=1, keepdims=True)
        return jnp.sum(jnp.where(spot, column, 0.0), axis=0, keepdims=True)

    def to_column(row):
        return jnp.sum(jnp.where(spot, row, 0.0), axis=1, keepdims=True)

    await_bytes(static_in, recv_sems.at[1])

    def masked(row, keep):
        return jnp.where(own & keep, row, 0.0)

    grid_y = 2 * dp + (lane - 32) // 32
    grid_z = lane % 32
    up_x = masked(face_x, jnp.broadcast_to(cell < CELL - 1, (1, LANES)))
    low_x = masked(static_in[0, 1:2, :], jnp.broadcast_to(cell > 0, (1, LANES)))
    up_y = masked(face_y, grid_y < GY - 1)
    low_y = masked(pltpu.roll(face_y, 32, 1), grid_y > 0)
    up_z = masked(face_z, grid_z < GZ - 1)
    low_z = masked(pltpu.roll(face_z, 1, 1), grid_z > 0)

    def roughness(row, lower, upper):
        return (
            up_x * (row - upper)
            + low_x * (row - lower)
            + up_y * (row - pltpu.roll(row, 96, 1))
            + low_y * (row - pltpu.roll(row, 32, 1))
            + up_z * (row - pltpu.roll(row, 127, 1))
            + low_z * (row - pltpu.roll(row, 1, 1))
        )

    residual = to_row(gradient_sum) - roughness(cond_row, static_in[0, 0:1, :], static_in[1, 0:1, :])
    residual = jnp.where(own, residual, 0.0)

    quarter = core + 2 * (cell % 2)
    weights = jnp.concatenate([setup_in[block, 4:5, :] for block in range(DP)], axis=0)

    def finish_step(step, held):
        await_bytes(scalar_in.at[step, pl.ds(63, 7)], recv_sems.at[2 + 5 * step + 4])
        sums = held["scalars"] + jnp.sum(scalar_in[step, 63:70], axis=0)
        norm, energy = sums[:, 0:1], sums[:, 1:2]
        predicted, rough, whole = held["image"], held["rough"], held["plane"]
        ratio = None
        if step > 0:
            ratio = norm / held["norm"]
            energy = energy + ratio * (2.0 * sums[:, 2:3] + ratio * held["energy"])
            predicted = predicted + ratio * held["predicted"]
            rough = rough + ratio * held["direction_rough"]
            whole = whole + ratio * held["whole"]
        square = jnp.sum(weights * predicted * predicted, axis=0, keepdims=True)
        length = norm / (energy + lane_sum(square))
        update, change = length * whole, length * predicted
        if step > 0:
            update, change = held["update"] + update, held["change"] + change
        held.update(
            norm=norm,
            energy=energy,
            predicted=predicted,
            direction_rough=rough,
            whole=whole,
            update=update,
            change=change,
        )
        return ratio, length

    def along(name, value, ratio, held):
        held[name] = value if ratio is None else value + ratio * held[name]
        return held[name]

    held = {}
    vector = residual
    for it in range(ITERS):
        sem = 2 + 5 * it
        halo_out[it] = vector
        for slot, (to_dp, to_cell) in enumerate(
            (
                (dp, above),
                (dp, below),
                ((dp + 1) % DP, cell),
                ((dp + DP - 1) % DP, cell),
            )
        ):
            push(
                halo_out.at[it],
                halo_in.at[it, slot],
                send_sems.at[sem],
                recv_sems.at[sem],
                to_dp,
                to_cell,
            )
        column = jnp.broadcast_to(to_column(vector), (OWN, LANES))
        for part in range(4):
            first_out[it, part] = jnp.concatenate(
                [
                    jnp.sum(sens[4 * part + row] * column, axis=0, keepdims=True)
                    for row in range(4)
                ],
                axis=0,
            )
        for slot, (to_core, to_x, to_y) in enumerate(PLANE):
            to_dp = 2 * chip + (core + to_core) % 2
            to_cell = (cell // 8 + to_x) % 4 * 8 + (cell + to_y) % 8
            push(
                first_out.at[it, to_dp % 2 + 2 * (to_cell % 2)],
                first_in.at[it, slot],
                send_sems.at[sem + 1],
                recv_sems.at[sem + 1],
                to_dp,
                to_cell,
            )

        if it > 0:
            ratio, length = finish_step(it - 1, held)
            residual = residual - length * along("hessian", vector, ratio, held)

        await_bytes(halo_in.at[it], recv_sems.at[sem])
        before, after = halo_in[it, 2], halo_in[it, 3]
        wide = jnp.where(own, vector, pltpu.roll(jnp.where(lane >= 64, before, after), 64, 1))
        rough = roughness(wide, halo_in[it, 0], halo_in[it, 1]) + DAMPING * vector
        if it > 0:
            rough = held["rough"] - length * along("hessian_rough", rough, ratio, held)
        held["rough"] = rough
        scalars = jnp.where(lane == 0, lane_sum(residual * residual), 0.0)
        scalars = jnp.where(lane == 1, lane_sum(residual * rough), scalars)
        if it > 0:
            scalars = jnp.where(lane == 2, lane_sum(residual * held["direction_rough"]), scalars)
        scalar_out[it, 0] = scalars
        for slot, (to_core, to_x, to_y) in enumerate(PLANE):
            push(
                scalar_out.at[it, 0],
                scalar_in.at[it, slot],
                send_sems.at[sem + 3],
                recv_sems.at[sem + 3],
                2 * chip + (core + to_core) % 2,
                (cell // 8 + to_x) % 4 * 8 + (cell + to_y) % 8,
            )

        await_bytes(first_in.at[it], recv_sems.at[sem + 1])
        partial = first_out[it, quarter] + jnp.sum(first_in[it], axis=0)
        second_in[it, 4 * chip + quarter] = jnp.concatenate([partial, residual], axis=0)
        for to_z, to_core, to_pair in COLUMN:
            push(
                second_in.at[it, 4 * chip + quarter],
                second_in.at[it, 4 * chip + quarter],
                send_sems.at[sem + 2],
                recv_sems.at[sem + 2],
                (chip + to_z) % 8 * 2 + (core + to_core) % 2,
                cell + to_pair * (1 - 2 * (cell % 2)),
            )

        await_bytes(scalar_in.at[it, pl.ds(0, 63)], recv_sems.at[sem + 3])
        scalars = scalars + jnp.sum(scalar_in[it, 0:63], axis=0)
        scalar_out[it, 1] = scalars
        for slot, to_z in enumerate((4, 3, 5, 2, 6, 1, 7)):
            push(
                scalar_out.at[it, 1],
                scalar_in.at[it, 63 + slot],
                send_sems.at[sem + 4],
                recv_sems.at[sem + 4],
                (chip + to_z) % 8 * 2 + core,
                cell,
            )

        held["scalars"] = scalars

        await_bytes(second_in.at[it, pl.ds(0, 31)], recv_sems.at[sem + 2])
        quarters = [second_in[it, part] for part in range(4)]
        for plane in range(1, 8):
            for part in range(4):
                quarters[part] += second_in[it, 4 * plane + part]
        image = jnp.concatenate([rows[0:4] for rows in quarters], axis=0)
        if it > 0:
            image = held["image"] - length * along("hessian_image", image, ratio, held)
        held["image"] = image
        if it < ITERS - 1:
            weighted = weights * image
            spread = sens[0] * weighted[0:1]
            for block in range(1, DP):
                spread += sens[block] * weighted[block : block + 1]
            vector = jnp.where(own, to_row(spread) + rough, 0.0)
        mine = [
            second_in[it, source // 2 * 4 + source % 2 + 2 * (cell % 2)][4:5]
            for source in range(DP)
        ]
        left = pltpu.roll(jnp.concatenate(mine[0::2], axis=0), 96, 1)
        right = pltpu.roll(jnp.concatenate(mine[1::2], axis=0), 32, 1)
        held["plane"] = jnp.where(lane < 64, left, right)

    finish_step(ITERS - 1, held)
    update, change = held["update"], held["change"]
    update_out[...] = update
    mine = lax.broadcasted_iota(jnp.int32, (DP, LANES), 0) == dp
    change_out[...] = jnp.sum(jnp.where(mine, change, 0.0), axis=0, keepdims=True)

    await_bytes(setup_in.at[pl.ds(0, DP - 1)], send_sems.at[0])
    await_bytes(static_in, send_sems.at[1])
    await_bytes(field_in.at[pl.ds(0, DP - 1)], field_send)
    for it in range(ITERS):
        sem = 2 + 5 * it
        await_bytes(halo_in.at[it], send_sems.at[sem])
        await_bytes(first_in.at[it], send_sems.at[sem + 1])
        await_bytes(second_in.at[it, pl.ds(0, 31)], send_sems.at[sem + 2])
        await_bytes(scalar_in.at[it, pl.ds(0, 63)], send_sems.at[sem + 3])
        await_bytes(scalar_in.at[it, pl.ds(63, 7)], send_sems.at[sem + 4])


def hand_on_kernel(update, change, update_out, change_out):
    update_out[...] = update[...]
    change_out[...] = change[...]


def per_device(configs, pole_fields, misfit, data_weight, conductivity, face_weights):
    vmem = pl.BlockSpec(memory_space=pltpu.VMEM)
    update, change = pl.pallas_call(
        kernel,
        name="inversion",
        out_shape=(
            jax.ShapeDtypeStruct((8, LANES), F32),
            jax.ShapeDtypeStruct((1, LANES), F32),
        ),
        in_specs=[pl.BlockSpec(memory_space=pltpu.HBM)] * 6,
        out_specs=(vmem, vmem),
        scratch_shapes=[
            pltpu.VMEM((3, POLE_ROWS, 8 * LANES), BF16),
            pltpu.VMEM((4, LANES), jnp.int32),
            pltpu.VMEM((1, LANES), F32),
            pltpu.VMEM((1, LANES), F32),
            pltpu.VMEM((8, LANES), F32),
            pltpu.VMEM((3, 8 * LANES), F32),
            pltpu.VMEM((DP, 3 * OWN, POLE_ROWS), BF16),
            pltpu.VMEM((DP, 3 * OWN, POLE_ROWS), BF16),
            pltpu.VMEM((CHUNK, 2 * DATA), BF16),
            pltpu.VMEM((CHUNK, 2 * DATA), BF16),
            pltpu.VMEM((3 * OWN, 2 * DATA), F32),
            pltpu.VMEM((DP, OWN, LANES), F32),
            pltpu.VMEM((8, LANES), F32),
            pltpu.VMEM((DP, 8, LANES), F32),
            pltpu.VMEM((2, LANES), F32),
            pltpu.VMEM((2, 2, LANES), F32),
            pltpu.VMEM((ITERS, 1, LANES), F32),
            pltpu.VMEM((ITERS, 4, 1, LANES), F32),
            pltpu.VMEM((ITERS, 4, 4, LANES), F32),
            pltpu.VMEM((ITERS, 63, 4, LANES), F32),
            pltpu.VMEM((ITERS, 32, 5, LANES), F32),
            pltpu.VMEM((ITERS, 2, 1, LANES), F32),
            pltpu.VMEM((ITERS, 70, 1, LANES), F32),
            pltpu.SemaphoreType.DMA,
            pltpu.SemaphoreType.DMA((DP,)),
            pltpu.SemaphoreType.DMA((2 + 5 * ITERS,)),
            pltpu.SemaphoreType.DMA((2 + 5 * ITERS,)),
            pltpu.SemaphoreType.DMA((6,)),
        ],
        compiler_params=pltpu.CompilerParams(
            collective_id=0, has_side_effects=True, vmem_limit_bytes=60 * 1024 * 1024
        ),
    )(
        pole_fields,
        configs.T,
        misfit.reshape(1, LANES),
        data_weight.reshape(1, LANES),
        conductivity.reshape(8, LANES),
        face_weights,
    )
    hand_on = pl.pallas_call(
        hand_on_kernel,
        name="results",
        out_shape=(
            jax.ShapeDtypeStruct((8, LANES), F32),
            jax.ShapeDtypeStruct((1, LANES), F32),
        ),
        in_specs=[pl.BlockSpec(memory_space=pltpu.VMEM)] * 2,
        out_specs=(pl.BlockSpec(memory_space=pltpu.VMEM),) * 2,
        scratch_shapes=[],
    )
    update, change = hand_on(update, change)
    return update.reshape(-1), change.reshape(-1)


def solution(mesh):
    placed = (P("dp", None), P(None, "dp", "cell"), P("dp"), P("dp"), P("cell"), P(None, "cell"))
    return jax.shard_map(
        per_device, mesh=mesh, in_specs=placed, out_specs=(P("cell"), P("dp")), check_vma=False
    )
```
